32 devices in a mesh: blk: 8 (over z, y), tp: 4 (over x, core).
Axes of the slice: x: 2, y: 2, z: 4, core: 2. Of those that a mesh axis runs over, the one named last changes fastest.
Arguments:
- patches: bfloat16 [1024, 1152], P('blk'), may hold values from -6 to 6
- latents: bfloat16 [512, 4096], P('blk'), may hold values from -6 to 6
- image_patches: int32 [8], replicated, may hold values from 1 to 512, as said below
- span_order: int32 [8], replicated, may hold values from 0 to 7, as said below
- vis_gains: float32 [2, 1152], replicated, may hold values from 0.5 to 1.5
- vis_shifts: float32 [2, 1152], replicated, may hold values from -1.75 to 1.75
- vis_qkv: bfloat16 [1152, 3, 1152], P('blk', None, 'tp'), may hold values from -0.1875 to 0.1875
- vis_qv_bias: float32 [2, 1152], P(None, 'tp'), may hold values from -1.75 to 1.75
- vis_out: bfloat16 [1152, 1152], P('tp', 'blk'), may hold values from -0.75 to 0.75
- vis_out_bias: float32 [2, 1152], replicated, may hold values from -1.75 to 1.75
- vis_fc1: bfloat16 [1152, 4304], P('blk', 'tp'), may hold values from -0.1875 to 0.1875
- vis_fc1_bias: float32 [4304], P('tp'), may hold values from -1.75 to 1.75
- vis_fc2: bfloat16 [4304, 1152], P('tp', 'blk'), may hold values from -0.09375 to 0.09375
- proj_gate_up: bfloat16 [1152, 2, 14336], P('blk', None, 'tp'), may hold values from -0.1875 to 0.1875
- proj_down: bfloat16 [14336, 4096], P('tp', 'blk'), may hold values from -0.046875 to 0.046875
- res_gains: float32 [4, 4096], replicated, may hold values from 0.5 to 1.5
- res_q: bfloat16 [4096, 1536], P('blk', 'tp'), may hold values from -0.09375 to 0.09375
- res_kv: bfloat16 [4096, 2, 384], P('blk', None, 'tp'), may hold values from -0.09375 to 0.09375
- res_out: bfloat16 [1536, 4096], P('tp', 'blk'), may hold values from -0.625 to 0.625
- res_gate_up: bfloat16 [4096, 2, 16384], P(None, None, ('blk', 'tp')), may hold values from -0.09375 to 0.09375
- res_down: bfloat16 [16384, 4096], P(('blk', 'tp')), may hold values from -0.046875 to 0.046875
- out_grad: bfloat16 [512, 4096], P('blk'), may hold values from -6 to 6
Outputs:
- latents_out: float32 [512, 4096], P('blk')
- patches_grad: float32 [1024, 1152], P('blk')
- latents_grad: float32 [512, 4096], P('blk')
- grad_vis_gains: float32 [2, 1152], replicated
- grad_vis_shifts: float32 [2, 1152], replicated
- grad_vis_qkv: float32 [1152, 3, 1152], P('blk', None, 'tp')
- grad_vis_qv_bias: float32 [2, 1152], P(None, 'tp')
- grad_vis_out: float32 [1152, 1152], P('tp', 'blk')
- grad_vis_out_bias: float32 [2, 1152], replicated
- grad_vis_fc1: float32 [1152, 4304], P('blk', 'tp')
- grad_vis_fc1_bias: float32 [4304], P('tp')
- grad_vis_fc2: float32 [4304, 1152], P('tp', 'blk')
- grad_proj_gate_up: float32 [1152, 2, 14336], P('blk', None, 'tp')
- grad_proj_down: float32 [14336, 4096], P('tp', 'blk')
- grad_res_gains: float32 [4, 4096], replicated
- grad_res_q: float32 [4096, 1536], P('blk', 'tp')
- grad_res_kv: float32 [4096, 2, 384], P('blk', None, 'tp')
- grad_res_out: float32 [1536, 4096], P('tp', 'blk')
- grad_res_gate_up: float32 [4096, 2, 16384], P(None, None, ('blk', 'tp'))
- grad_res_down: float32 [16384, 4096], P(('blk', 'tp'))
The draws below stay inside these ranges and needn't reach their ends.
Inputs may be any that keep to these rules, and one draw needn't show every extreme that they name: `image_patches`: the counts sum to 1024; image 0 has 512 patches, every other image fewer. `span_order`: each span is held by exactly one index of blk; index 0 holds span 0, index 7 holds span 1 and index 4 holds span 2.
All inputs are finite; a program needn't handle non-finite values.
Results may differ from the reference program's by a relative error of at most 0.04.
Values may be sent and summed in bfloat16 or wider, within the bound.
No kernel may reach another device: no remote copies, remote signals or barrier semaphores. Data moves between devices by JAX's collectives and lax.ppermute only.
A program may use at most 384 MiB of HBM per device.

```python
import jax
import jax.numpy as jnp
import numpy as np
from jax import lax

HEADS = 16
HEAD_VIS = 72
D_VIS = 1152
FF_VIS = 4304
FF_PROJ = 14336
D_TEXT = 4096
RES_HEADS = 16
RES_HEAD = 96
KV_HEADS = 4
FF_RES = 16384
LATENTS = 64
TOK_BLK = 128
SPANS = 8
TOKENS = 1024
IMAGES = 8
LAT_BLK = 64
LAT = 512
BIG_DOC = 512
N_BLK = 8


def draw_image_patches(key, part):
    key = jax.random.fold_in(key, 11)
    small_count = IMAGES - 1
    remaining = TOKENS - BIG_DOC
    middle = remaining // small_count
    leftover = remaining - middle * small_count
    shifts = jax.random.randint(key, (small_count,), 0, middle // 2 + 1).astype(jnp.int32)
    counts = middle + shifts - jnp.roll(shifts, -1)
    counts = counts.at[small_count - 1].add(leftover)
    return jnp.concatenate([jnp.full((1,), BIG_DOC, jnp.int32), counts.astype(jnp.int32)])


def draw_span_order(key, part):
    key = jax.random.fold_in(key, 23)
    spare = np.array([device for device in range(SPANS) if device not in (0, SPANS // 2, SPANS - 1)], dtype=np.int32)
    filler = jax.random.permutation(key, SPANS - 3).astype(jnp.int32) + 3
    order = jnp.zeros((SPANS,), jnp.int32).at[spare].set(filler)
    order = order.at[SPANS - 1].set(1).at[SPANS // 2].set(2)
    return order.astype(jnp.int32)


def level_of(own_key, dims, cuts, least, high):
    level = 1.0
    for axis_at, shards_of in cuts:
        heights = jax.random.uniform(jax.random.fold_in(jax.random.fold_in(own_key, 6), axis_at), (shards_of,), jnp.float32, least / len(cuts), high / len(cuts))
        level = level * jnp.repeat(jnp.exp(heights), dims[axis_at] // shards_of).reshape((-1,) + (1,) * (len(dims) - 1 - axis_at))
    return level


def gaussian(key, dims, scale, reach, pieces=(), held_as=jnp.bfloat16):
    level = level_of(key, dims, pieces, -0.22, 0.18) if pieces else 1.0
    entries = jax.random.normal(key, dims, jnp.float32) * scale * level
    return jnp.minimum(jnp.maximum(entries, -reach), reach).astype(held_as)


def setup_inputs(seed: int = 0) -> dict:
    key_of = jax.random.split(jax.random.key(seed), 23)
    patches = gaussian(key_of[0], (TOKENS, D_VIS), 1.0, 6.0, ((0, 8),))
    latents = gaussian(key_of[1], (LAT, D_TEXT), 1.0, 6.0, ((0, 8),))
    image_patches = draw_image_patches(jax.random.fold_in(key_of[22], 71), 0)
    span_order = draw_span_order(jax.random.fold_in(key_of[22], 71), 0)
    vis_gains = jnp.clip(1.0 + 0.1 * jax.random.normal(key_of[4], (2, D_VIS), jnp.float32), 0.5, 1.5)
    vis_shifts = gaussian(key_of[5], (2, D_VIS), 0.3, 1.75, (), jnp.float32)
    vis_qkv = gaussian(key_of[6], (D_VIS, 3, D_VIS), D_VIS ** -0.5, 0.1875, ((0, 8), (2, 4)))
    vis_qv_bias = gaussian(key_of[7], (2, D_VIS), 0.3, 1.75, ((1, 4),), jnp.float32)
    vis_out = gaussian(key_of[8], (D_VIS, D_VIS), (D_VIS // 16) ** -0.5, 0.75, ((0, 4), (1, 8)))
    vis_out_bias = gaussian(key_of[9], (2, D_VIS), 0.3, 1.75, (), jnp.float32)
    vis_fc1 = gaussian(key_of[10], (D_VIS, FF_VIS), D_VIS ** -0.5, 0.1875, ((0, 8), (1, 4)))
    vis_fc1_bias = gaussian(key_of[11], (FF_VIS,), 0.3, 1.75, ((0, 4),), jnp.float32)
    vis_fc2 = gaussian(key_of[12], (FF_VIS, D_VIS), FF_VIS ** -0.5, 0.09375, ((0, 4), (1, 8)))
    proj_gate_up = gaussian(key_of[13], (D_VIS, 2, FF_PROJ), D_VIS ** -0.5, 0.1875, ((0, 8), (2, 4)))
    proj_down = gaussian(key_of[14], (FF_PROJ, D_TEXT), FF_PROJ ** -0.5, 0.046875, ((0, 4), (1, 8)))
    res_gains = jnp.clip(1.0 + 0.1 * jax.random.normal(key_of[15], (4, D_TEXT), jnp.float32), 0.5, 1.5)
    res_q = gaussian(key_of[16], (D_TEXT, RES_HEADS * RES_HEAD), D_TEXT ** -0.5, 0.09375, ((0, 8), (1, 4)))
    res_kv = gaussian(key_of[17], (D_TEXT, 2, KV_HEADS * RES_HEAD), D_TEXT ** -0.5, 0.09375, ((0, 8), (2, 4)))
    res_out = gaussian(key_of[18], (RES_HEADS * RES_HEAD, D_TEXT), (RES_HEADS * RES_HEAD // 16) ** -0.5, 0.625, ((0, 4), (1, 8)))
    res_gate_up = gaussian(key_of[19], (D_TEXT, 2, FF_RES), D_TEXT ** -0.5, 0.09375, ((2, 32),))
    res_down = gaussian(key_of[20], (FF_RES, D_TEXT), FF_RES ** -0.5, 0.046875, ((0, 32),))
    out_grad = gaussian(key_of[21], (LAT, D_TEXT), 1.0, 6.0, ((0, 8),))
    return {"patches": patches, "latents": latents, "image_patches": image_patches, "span_order": span_order, "vis_gains": vis_gains, "vis_shifts": vis_shifts, "vis_qkv": vis_qkv, "vis_qv_bias": vis_qv_bias, "vis_out": vis_out, "vis_out_bias": vis_out_bias, "vis_fc1": vis_fc1, "vis_fc1_bias": vis_fc1_bias, "vis_fc2": vis_fc2, "proj_gate_up": proj_gate_up, "proj_down": proj_down, "res_gains": res_gains, "res_q": res_q, "res_kv": res_kv, "res_out": res_out, "res_gate_up": res_gate_up, "res_down": res_down, "out_grad": out_grad}


EPSILON = 1e-06
HIGHEST = lax.Precision.HIGHEST

@jax.custom_vjp
def low(v):
    return lax.optimization_barrier(v.astype(jnp.bfloat16)).astype(jnp.float32)

@jax.custom_vjp
def low_back(v):
    return v

def low_keep(v):
    return (low(v), None)

def low_pass(kept, grad):
    return (grad,)

def back_keep(v):
    return (v, None)

def back_low(kept, grad):
    return (low(grad),)
low.defvjp(low_keep, low_pass)
low_back.defvjp(back_keep, back_low)

def layer_norm(values, gain, shift):
    center = values - lax.optimization_barrier(jnp.mean(values, axis=-1, keepdims=True))
    spread = lax.optimization_barrier(jnp.mean(center * center, axis=-1, keepdims=True))
    return center * lax.rsqrt(spread + EPSILON) * gain + shift

def rms_norm(values, gain):
    return values * lax.rsqrt(lax.optimization_barrier(jnp.mean(values * values, axis=-1, keepdims=True)) + EPSILON) * gain

def gelu_tanh(values):
    return jax.nn.gelu(values, approximate=True)

def swiglu(gate_part, up_part):
    return jax.nn.silu(gate_part) * up_part

def matmul_high(left, right):
    return jnp.dot(left, right, precision=HIGHEST)

def patch_images(image_patches, span_order):
    bounds = jnp.cumsum(image_patches).astype(jnp.int32)
    offsets = jnp.arange(TOK_BLK, dtype=jnp.int32)
    stream = (span_order[:, None] * TOK_BLK + offsets[None, :]).reshape(-1)
    return lax.optimization_barrier(jnp.sum((stream[:, None] >= bounds[None, :]).astype(jnp.int32), axis=1))

def vision_attention(query_rows, key_rows, value_rows, image_ids):
    query_heads = query_rows.reshape(TOKENS // TOK_BLK, TOK_BLK, HEADS, HEAD_VIS)
    key_heads = key_rows.reshape(TOKENS, HEADS, HEAD_VIS)
    value_heads = value_rows.reshape(TOKENS, HEADS, HEAD_VIS)
    id_blocks = image_ids.reshape(TOKENS // TOK_BLK, TOK_BLK)

    def block(block_pair):
        query_block, id_block = block_pair
        scores = jnp.einsum('qhd,khd->hqk', query_block, key_heads, precision=HIGHEST) * HEAD_VIS ** (-0.5)
        scores = low_back(scores)
        allowed = id_block[:, None] == image_ids[None, :]
        weights = jax.nn.softmax(jnp.where(allowed[None], scores, -jnp.inf), axis=-1)
        return jnp.einsum('hqk,khd->qhd', low(weights), value_heads, precision=HIGHEST)
    result = lax.map(jax.checkpoint(block), (query_heads, id_blocks))
    return result.reshape(TOKENS, HEADS * HEAD_VIS)

def latent_attention(query_rows, key_rows, value_rows, key_images):
    group_size = RES_HEADS // KV_HEADS
    query_heads = query_rows.reshape(N_BLK, LAT_BLK, KV_HEADS, group_size, RES_HEAD)
    key_heads = key_rows.reshape(-1, KV_HEADS, RES_HEAD)
    value_heads = value_rows.reshape(-1, KV_HEADS, RES_HEAD)
    query_images = (jnp.arange(LAT, dtype=jnp.int32) // LATENTS).reshape(N_BLK, LAT_BLK)

    def block(block_pair):
        query_block, image_block = block_pair
        scores = jnp.einsum('qkgd,nkd->kgqn', query_block, key_heads, precision=HIGHEST) * RES_HEAD ** (-0.5)
        scores = low_back(scores)
        allowed = image_block[:, None] == key_images[None, :]
        weights = jax.nn.softmax(jnp.where(allowed, scores, -jnp.inf), axis=-1)
        return jnp.einsum('kgqn,nkd->qkgd', low(weights), value_heads, precision=HIGHEST)
    result = lax.map(jax.checkpoint(block), (query_heads, query_images))
    return result.reshape(LAT, RES_HEADS * RES_HEAD)

def forward(image_ids, params):
    patches, latents, vis_gains, vis_shifts, vis_qkv, vis_qv_bias, vis_out, vis_out_bias, vis_fc1, vis_fc1_bias, vis_fc2, proj_gate_up, proj_down, res_gains, res_q, res_kv, res_out, res_gate_up, res_down = params
    attn_input = low(layer_norm(patches, vis_gains[0], vis_shifts[0]))
    projected = jnp.einsum('td,dje->tje', attn_input, vis_qkv, precision=HIGHEST)
    query_rows = low_back(low(projected[:, 0] + vis_qv_bias[0]))
    key_rows = low_back(low(projected[:, 1]))
    value_rows = low_back(low(projected[:, 2] + vis_qv_bias[1]))
    attended = low_back(low(vision_attention(query_rows, key_rows, value_rows, image_ids)))
    hidden_one = patches + low_back(matmul_high(attended, vis_out) + vis_out_bias[0])
    mlp_input = low(layer_norm(hidden_one, vis_gains[1], vis_shifts[1]))
    fc1_pre = low_back(matmul_high(mlp_input, vis_fc1) + vis_fc1_bias)
    fc1_low = low(gelu_tanh(fc1_pre))
    vision_out = hidden_one + low_back(matmul_high(fc1_low, vis_fc2) + vis_out_bias[1])
    vision_low = low(vision_out)
    gate_up = jnp.einsum('td,dje->tje', vision_low, proj_gate_up, precision=HIGHEST)
    proj_low = low(swiglu(low_back(gate_up[:, 0]), low_back(gate_up[:, 1])))
    context = low_back(matmul_high(proj_low, proj_down))
    context_low = low(rms_norm(context, res_gains[0]))
    patch_kv = low_back(low(jnp.einsum('td,dje->tje', context_low, res_kv, precision=HIGHEST)))
    latent_low = low(rms_norm(latents, res_gains[1]))
    latent_query = low_back(low(matmul_high(latent_low, res_q)))
    latent_kv = low_back(low(jnp.einsum('td,dje->tje', latent_low, res_kv, precision=HIGHEST)))
    key_all = jnp.concatenate([patch_kv[:, 0], latent_kv[:, 0]], axis=0)
    value_all = jnp.concatenate([patch_kv[:, 1], latent_kv[:, 1]], axis=0)
    latent_images = jnp.arange(LAT, dtype=jnp.int32) // LATENTS
    key_images = jnp.concatenate([image_ids, latent_images]).astype(jnp.int32)
    res_result = low_back(low(latent_attention(latent_query, key_all, value_all, key_images)))
    latent_one = latents + low_back(matmul_high(res_result, res_out))
    post_low = low(rms_norm(latent_one, res_gains[2]))
    gate_up_two = jnp.einsum('td,dje->tje', post_low, res_gate_up, precision=HIGHEST)
    mlp_low = low(swiglu(low_back(gate_up_two[:, 0]), low_back(gate_up_two[:, 1])))
    latent_two = latent_one + low_back(matmul_high(mlp_low, res_down))
    return rms_norm(latent_two, res_gains[3])

def reference(patches, latents, image_patches, span_order, vis_gains, vis_shifts, vis_qkv, vis_qv_bias, vis_out, vis_out_bias, vis_fc1, vis_fc1_bias, vis_fc2, proj_gate_up, proj_down, res_gains, res_q, res_kv, res_out, res_gate_up, res_down, out_grad):
    image_ids = patch_images(image_patches, span_order)
    floats = tuple((element.astype(jnp.float32) for element in (patches, latents, vis_gains, vis_shifts, vis_qkv, vis_qv_bias, vis_out, vis_out_bias, vis_fc1, vis_fc1_bias, vis_fc2, proj_gate_up, proj_down, res_gains, res_q, res_kv, res_out, res_gate_up, res_down)))

    def forward_ids(params):
        return forward(image_ids, params)
    result, pull_back = jax.vjp(forward_ids, floats)
    gradients = pull_back(out_grad.astype(jnp.float32))[0]
    return (result, gradients[0], gradients[1], gradients[2], gradients[3], gradients[4], gradients[5], gradients[6], gradients[7], gradients[8], gradients[9], gradients[10], gradients[11], gradients[12], gradients[13], gradients[14], gradients[15], gradients[16], gradients[17], gradients[18])
```

```python
import jax
import jax.numpy as jnp
from jax import lax
from jax.sharding import PartitionSpec as P

HEADS = 16
HEAD_VIS = 72
RES_HEAD = 96
LATENTS = 64
EPSILON = 1e-06
EVERY = ("blk", "tp")
BF = jnp.bfloat16
F32 = jnp.float32


def swap_core(value):
    return lax.ppermute(value, "tp", [(i, i ^ 1) for i in range(lax.axis_size("tp"))])


def swap_x(value):
    return lax.ppermute(value, "tp", [(i, i ^ 2) for i in range(lax.axis_size("tp"))])


def my_x():
    return lax.axis_index("tp") // 2


def my_core():
    return lax.axis_index("tp") % 2


def pick(flag, one, zero):
    return jnp.where(flag == 1, one, zero)


def exchange(chunks, axis):
    return lax.all_to_all(chunks, axis, 0, 0, tiled=True)


def gather_direct(value, axis, count):
    return exchange(jnp.broadcast_to(value[None], (count,) + value.shape), axis)


def sum_blk(partial):
    return jnp.sum(exchange(partial.astype(BF), "blk").astype(F32), axis=0)


def sum_tp_quarter(partial):
    pairs = partial.reshape((2, 2) + partial.shape[1:])
    core, x = my_core(), my_x()
    keep = pick(core, pairs[:, 1], pairs[:, 0])
    send = pick(core, pairs[:, 0], pairs[:, 1]).astype(BF)
    half = keep + swap_core(send).astype(F32)
    keep = pick(x, half[1], half[0])
    send = pick(x, half[0], half[1]).astype(BF)
    return keep + swap_x(send).astype(F32)


def gather_tp(value):
    other = swap_x(value)
    x, core = my_x(), my_core()
    both = pick(x, jnp.stack([other, value]), jnp.stack([value, other]))
    far = swap_core(both)
    quad = pick(core, jnp.stack([far, both], axis=1), jnp.stack([both, far], axis=1))
    return quad.reshape((4,) + value.shape)


def sum_tp(partial):
    chip = (partial + swap_core(partial)).astype(BF)
    return chip.astype(F32) + swap_x(chip).astype(F32)


def gather_blk(value):
    return gather_direct(value, "blk", lax.axis_size("blk"))


def gather_blk_later(value):
    return lax.all_gather(value, "blk", axis=0, tiled=False)


def gather_every(value):
    return gather_tp(gather_blk(value))


def sum_every(partial):
    return sum_blk(sum_tp_quarter(partial))


def sum_small(rows):
    blk, tp = lax.axis_size("blk"), lax.axis_size("tp")
    count = blk * tp
    width = rows.shape[0]
    unit = count * 128
    padded = jnp.pad(rows, (0, (-width) % unit)).reshape(count, -1)
    own = jnp.sum(exchange(padded, EVERY), axis=0)
    return gather_direct(own, EVERY, count).reshape(-1)[:width]


def layer_norm(values, gain, shift):
    center = values - jnp.mean(values, axis=-1, keepdims=True)
    spread = jnp.mean(center * center, axis=-1, keepdims=True)
    return center * lax.rsqrt(spread + EPSILON) * gain + shift


def rms_norm(values, gain):
    return values * lax.rsqrt(jnp.mean(values * values, axis=-1, keepdims=True) + EPSILON) * gain


def gelu_tanh(values):
    return jax.nn.gelu(values, approximate=True)


def swiglu(gate_part, up_part):
    return jax.nn.silu(gate_part) * up_part


def mm(spec, left, right):
    return jnp.einsum(spec, left, right, preferred_element_type=F32)


def dot(left, right, on_left, on_right):
    return lax.dot_general(
        left, right, (((on_left,), (on_right,)), ((), ())), preferred_element_type=F32
    )


def halves(value):
    high = lax.reduce_precision(value, 8, 7)
    return high, lax.reduce_precision(value - high, 8, 7)


def stream_images(image_patches, span_order, tok_rows):
    bounds = jnp.cumsum(image_patches)
    rows = span_order[:, None] * tok_rows + jnp.arange(tok_rows, dtype=jnp.int32)[None, :]
    stream = rows.reshape(-1)
    return jnp.sum((stream[:, None] >= bounds[None, :]).astype(jnp.int32), axis=1)


def per_device(
    patches,
    latents,
    image_patches,
    span_order,
    vis_gains,
    vis_shifts,
    vis_qkv,
    vis_qv_bias,
    vis_out,
    vis_out_bias,
    vis_fc1,
    vis_fc1_bias,
    vis_fc2,
    proj_gate_up,
    proj_down,
    res_gains,
    res_q,
    res_kv,
    res_out,
    res_gate_up,
    res_down,
    out_grad,
):
    blk = lax.axis_size("blk")
    b, t = lax.axis_index("blk"), lax.axis_index("tp")
    tok, wide = patches.shape
    lat, text = latents.shape
    sub, lsub = tok // 4, lat // 4
    tokens, lats = tok * blk, lat * blk
    wcol, tcol = wide // blk, text // blk
    heads = HEADS // 4
    unit = proj_down.shape[0] // blk
    hidden = proj_down.shape[0]
    qcols = res_q.shape[1]
    kvcols = RES_HEAD

    qkv_shard = vis_qkv.transpose(1, 0, 2)
    qkv_full = gather_blk_later(qkv_shard)
    qkv_full = qkv_full.transpose(1, 0, 2, 3).reshape(3, wide, -1)
    gu_chunks = proj_gate_up.reshape(wcol, 2, blk, unit).transpose(2, 1, 0, 3)
    gu_own = exchange(gu_chunks, "blk").transpose(1, 0, 2, 3).reshape(2, wide, unit)
    out_full = gather_blk_later(vis_out.T).reshape(wide, -1)
    fc1_full = gather_blk_later(vis_fc1).reshape(wide, -1)
    fc2_full = gather_blk_later(vis_fc2.T).reshape(wide, -1)
    rout_full = gather_blk_later(res_out.T).reshape(text, -1)
    rkv_own = res_kv.reshape(tcol, 2 * kvcols)
    rkv_quad = gather_tp(rkv_own)

    latent_in = latents.astype(F32)
    latent_low = rms_norm(latent_in, res_gains[1]).astype(BF)
    latent_cols = exchange(latent_low.reshape(lat, blk, tcol).transpose(1, 0, 2), "blk")
    latent_cols = latent_cols.reshape(lats, tcol)
    latent_qkv = sum_blk(
        jnp.concatenate([dot(latent_cols, res_q, 1, 0), dot(latent_cols, rkv_own, 1, 0)], axis=1)
        .astype(BF)
        .reshape(blk, lat, qcols + 2 * kvcols)
    ).astype(BF)
    latent_query = latent_qkv[:, :qcols]
    latent_kv = latent_qkv[:, qcols:]

    all_images = stream_images(image_patches, span_order, tok)
    own_images = lax.dynamic_slice_in_dim(all_images, b * tok, tok)
    allowed_vis = own_images[:, None] == all_images[None, :]
    inputs = patches.astype(F32)
    normed_one, norm_one_pull = jax.vjp(layer_norm, inputs, vis_gains[0], vis_shifts[0])
    attn_input = normed_one.astype(BF)
    attn_cols = exchange(attn_input.reshape(tok, blk, wcol).transpose(1, 0, 2), "blk")
    attn_cols = attn_cols.reshape(tokens, wcol)
    query_rows = (dot(attn_input, qkv_full[0], 1, 0) + vis_qv_bias[0]).astype(BF)
    key_rows = dot(attn_input, qkv_full[1], 1, 0).astype(BF)
    value_rows = (dot(attn_input, qkv_full[2], 1, 0) + vis_qv_bias[1]).astype(BF)
    kv_all = gather_blk(jnp.stack([key_rows, value_rows]))
    query_all = gather_blk_later(query_rows).reshape(tokens, heads, HEAD_VIS)
    key_all = kv_all[:, 0].reshape(tokens, heads, HEAD_VIS)
    value_all = kv_all[:, 1].reshape(tokens, heads, HEAD_VIS)
    query_heads = query_rows.reshape(tok, heads, HEAD_VIS)
    key_heads = key_rows.reshape(tok, heads, HEAD_VIS)
    value_heads = value_rows.reshape(tok, heads, HEAD_VIS)
    vis_scale = HEAD_VIS ** (-0.5)
    scores = mm("qhd,khd->hqk", query_heads, key_all) * vis_scale
    scores = jnp.where(allowed_vis[None], scores, -jnp.inf)
    row_top = jnp.max(scores, axis=-1)
    weights = jnp.exp(scores - row_top[..., None])
    weight_sum = jnp.sum(weights, axis=-1)
    weighted = mm("hqk,khd->hqd", weights.astype(BF), value_all)
    vis_lse = row_top + jnp.log(weight_sum)
    vis_result = (weighted / weight_sum[..., None]).transpose(1, 0, 2)
    attn_output = vis_result.astype(BF).reshape(tok, -1)

    hidden_one = inputs + sum_tp(dot(attn_output, out_full, 1, 1)) + vis_out_bias[0]
    normed_two, norm_two_pull = jax.vjp(layer_norm, hidden_one, vis_gains[1], vis_shifts[1])
    mlp_input = normed_two.astype(BF)
    mlp_cols = exchange(mlp_input.reshape(tok, blk, wcol).transpose(1, 0, 2), "blk")
    mlp_cols = mlp_cols.reshape(tokens, wcol)
    fc1_pre = dot(mlp_input, fc1_full, 1, 0) + vis_fc1_bias
    fc1_act, gelu_pull = jax.vjp(gelu_tanh, fc1_pre)
    fc1_low = fc1_act.astype(BF)
    fc2_part = dot(fc1_low, fc2_full, 1, 1).reshape(4, sub, wide)
    hidden_sub = lax.dynamic_slice_in_dim(hidden_one, t * sub, sub)
    vision_sub = hidden_sub + sum_tp_quarter(fc2_part) + vis_out_bias[1]
    vision_low = gather_every(vision_sub.astype(BF)).reshape(tokens, wide)
    attn_out_all = gather_blk_later(attn_output).reshape(tokens, -1)
    fc1_low_all = gather_blk_later(fc1_low).reshape(tokens, -1)

    gate = dot(vision_low, gu_own[0], 1, 0)
    up = dot(vision_low, gu_own[1], 1, 0)
    proj_hidden, proj_pull = jax.vjp(swiglu, gate, up)
    proj_all = gather_blk_later(proj_hidden.astype(BF))
    pdown = proj_down.reshape(blk, unit, tcol)
    context_part = mm("bth,bhc->tc", proj_all, pdown)
    quarter = tokens // 4
    context = sum_tp_quarter(context_part.reshape(4, quarter, tcol))
    gain_context_own = lax.dynamic_slice_in_dim(res_gains[0], b * tcol, tcol)
    scaled_low = (context * gain_context_own).astype(BF)
    kv_part = mm("kc,tcj->tkj", scaled_low, rkv_quad)
    square_part = jnp.sum(context * context, axis=-1)
    high, low = halves(square_part)
    stats = jnp.pad(jnp.stack([high, low], axis=1), ((0, 0), (0, 2 * kvcols - 2)))
    kv_sums = sum_blk(
        jnp.concatenate([kv_part, stats[None]], axis=0)
        .astype(BF)
        .reshape(5, blk, sub, 2 * kvcols)
        .transpose(1, 0, 2, 3)
    )
    scale_sub = lax.rsqrt((kv_sums[4, :, 0] + kv_sums[4, :, 1]) / text + EPSILON)
    patch_kv = (kv_sums[:4] * scale_sub[None, :, None]).astype(BF)
    patch_all = exchange(
        jnp.broadcast_to(patch_kv[None], (blk,) + patch_kv.shape).reshape(4 * blk, sub, -1), EVERY
    ).reshape(tokens, 2 * kvcols)

    latent_images = b * (lat // LATENTS) + jnp.arange(lat, dtype=jnp.int32) // LATENTS
    key_images = jnp.concatenate([all_images, latent_images])
    allowed_res = latent_images[:, None] == key_images[None, :]
    res_kv_all = jnp.concatenate([patch_all, latent_kv], axis=0)
    res_key, res_value = res_kv_all[:, :kvcols], res_kv_all[:, kvcols:]
    group = qcols // RES_HEAD
    res_query = latent_query.reshape(lat, group, RES_HEAD)
    res_scale = RES_HEAD ** (-0.5)
    res_scores = mm("qgd,nd->gqn", res_query, res_key) * res_scale
    res_scores = jnp.where(allowed_res[None], res_scores, -jnp.inf)
    res_top = jnp.max(res_scores, axis=-1)
    res_weights = jnp.exp(res_scores - res_top[..., None])
    res_sum = jnp.sum(res_weights, axis=-1)
    res_result = (
        mm("gqn,nd->gqd", res_weights.astype(BF), res_value) / res_sum[..., None]
    ).transpose(1, 0, 2)
    res_lse = res_top + jnp.log(res_sum)
    result_low = res_result.astype(BF).reshape(lat, qcols)

    latent_sub = lax.dynamic_slice_in_dim(latent_in, t * lsub, lsub)
    latent_one = latent_sub + sum_tp_quarter(
        dot(result_low, rout_full, 1, 1).reshape(4, lsub, text)
    )
    post_normed, post_pull = jax.vjp(rms_norm, latent_one, res_gains[2])
    post_all = gather_every(post_normed.astype(BF)).reshape(lats, text)
    result_all = gather_blk_later(result_low).reshape(lats, qcols)
    gate_up_two = mm("td,dje->tje", post_all, res_gate_up)
    mlp_hidden, mlp_pull = jax.vjp(swiglu, gate_up_two[:, 0], gate_up_two[:, 1])
    mlp_low = mlp_hidden.astype(BF)
    down_part = dot(mlp_low, res_down, 1, 0).reshape(4, blk, lsub, text)
    latent_two = latent_one + sum_every(down_part)
    final_normed, final_pull = jax.vjp(rms_norm, latent_two, res_gains[3])
    grad_sub = lax.dynamic_slice_in_dim(out_grad, t * lsub, lsub).astype(F32)
    dlatent_two, gain_final = final_pull(grad_sub)
    latents_out = gather_tp(final_normed).reshape(lat, text)

    dmlp_all = gather_every(dlatent_two.astype(BF)).reshape(lats, text)
    dgate_two, dup_two = mlp_pull(dot(dmlp_all, res_down, 1, 1))
    dgate_up_two = jnp.stack([dgate_two, dup_two], axis=1).astype(BF)
    dpost_part = mm("tje,dje->td", dgate_up_two, res_gate_up).reshape(4, blk, lsub, text)
    dpost = sum_every(dpost_part)
    grad_res_down = dot(mlp_low, dmlp_all, 0, 0)
    grad_res_gate_up = mm("td,tje->dje", post_all, dgate_up_two)
    dlatent_part, gain_post = post_pull(dpost)
    dlatent_one = dlatent_two + dlatent_part
    dattn_low = gather_tp(dlatent_one.astype(BF)).reshape(lat, text)

    dresult = dot(dattn_low, rout_full, 1, 0).astype(BF)
    dresult_heads = dresult.reshape(lat, group, RES_HEAD)
    res_delta = jnp.sum(dresult_heads.astype(F32) * res_result, axis=-1).T
    res_prob = jnp.exp(res_scores - res_lse[..., None])
    dprob = mm("qgd,nd->gqn", dresult_heads, res_value)
    dscores = (res_prob * (dprob - res_delta[..., None])).astype(BF)
    dquery = mm("gqn,nd->qgd", dscores, res_key) * res_scale
    dkey = mm("gqn,qgd->nd", dscores, res_query) * res_scale
    dvalue = mm("gqn,qgd->nd", res_prob.astype(BF), dresult_heads)
    dquery_own = dquery.reshape(lat, qcols).astype(BF)
    dkv_low = jnp.concatenate([dkey, dvalue], axis=1).astype(BF)
    dpatch_local, dlatent_kv = dkv_low[:tokens], dkv_low[tokens:]
    dpatch_sub = jnp.sum(
        exchange(dpatch_local.reshape(4 * blk, sub, 2 * kvcols), EVERY)
        .reshape(blk, 4, sub, 2 * kvcols)
        .astype(F32),
        axis=0,
    )
    along = jnp.sum(dpatch_sub * patch_kv.astype(F32), axis=(0, 2)) / text
    a_high, a_low = halves(along)
    s_high, s_low = halves(scale_sub)
    row_stats = jnp.pad(
        jnp.stack([a_high, a_low, s_high, s_low], axis=1), ((0, 0), (0, 2 * kvcols - 4))
    )
    dpatch_rows = gather_blk(jnp.concatenate([dpatch_sub, row_stats[None]], axis=0).astype(BF))
    dpatch_rows = dpatch_rows.transpose(1, 0, 2, 3).reshape(5, quarter, 2 * kvcols)
    dpatch_quad = dpatch_rows[:4]
    along_rows = dpatch_rows[4, :, 0].astype(F32) + dpatch_rows[4, :, 1].astype(F32)
    scale_rows = dpatch_rows[4, :, 2].astype(F32) + dpatch_rows[4, :, 3].astype(F32)
    dcontext_normed = mm("tkj,tcj->kc", dpatch_quad, rkv_quad)
    unit_context = context * scale_rows[:, None]
    dcontext = scale_rows[:, None] * (
        dcontext_normed * gain_context_own - unit_context * along_rows[:, None]
    )
    gain_context = jnp.sum(dcontext_normed * unit_context, axis=0)
    context_low = (unit_context * gain_context_own).astype(BF)

    dcontext_low = gather_tp(dcontext.astype(BF)).reshape(tokens, tcol)
    dproj_part = mm("tc,bhc->bth", dcontext_low, pdown)
    dproj = sum_blk(dproj_part)
    dgate, dup = proj_pull(dproj)
    dgate_low, dup_low = dgate.astype(BF), dup.astype(BF)
    dvision_part = dot(dgate_low, gu_own[0], 1, 1) + dot(dup_low, gu_own[1], 1, 1)
    dvision_sub = sum_every(dvision_part.reshape(4, blk, sub, wide))
    dvision_out = gather_tp(dvision_sub).reshape(tok, wide)
    grad_proj_down = mm("bth,tc->bhc", proj_all, dcontext_low).reshape(hidden, tcol)
    grad_gu = jnp.stack([dot(vision_low, dgate_low, 0, 0), dot(vision_low, dup_low, 0, 0)])
    grad_gu = exchange(grad_gu.astype(BF).reshape(2, blk, wcol, unit).transpose(1, 0, 2, 3), "blk")
    grad_proj_gate_up = grad_gu.transpose(2, 1, 0, 3).reshape(wcol, 2, hidden).astype(F32)

    dqkv_rows = gather_blk_later(jnp.concatenate([dquery_own, dlatent_kv], axis=1))
    dqkv_rows = dqkv_rows.reshape(lats, qcols + 2 * kvcols)
    dquery_all, dlkv_all = dqkv_rows[:, :qcols], dqkv_rows[:, qcols:]
    grad_res_q = dot(latent_cols, dquery_all, 0, 0)
    grad_res_kv = dot(latent_cols, dlkv_all, 0, 0) + sum_tp_quarter(
        mm("kc,tkj->tcj", context_low, dpatch_quad)
    )
    grad_res_kv = grad_res_kv.reshape(tcol, 2, kvcols)
    dlatent_part = dot(dquery_all, res_q, 1, 1) + dot(dlkv_all, rkv_own, 1, 1)
    dlatent_rows = exchange(dlatent_part.astype(BF).reshape(4 * blk, lsub, tcol), EVERY)
    dlatent_normed = (
        jnp.sum(dlatent_rows.reshape(blk, 4, lsub, tcol).astype(F32), axis=1)
        .transpose(1, 0, 2)
        .reshape(lsub, text)
    )
    latent_pull = jax.vjp(rms_norm, latent_sub, res_gains[1])[1]
    dlatent_in, gain_latent = latent_pull(dlatent_normed)
    latents_grad = gather_tp(dlatent_one + dlatent_in).reshape(lat, text)
    dattn_cols = exchange(dattn_low.reshape(lat, blk, tcol).transpose(1, 0, 2), "blk")
    grad_res_out = dot(result_all, dattn_cols.reshape(lats, tcol), 0, 0)
    gain_context_full = lax.dynamic_update_slice_in_dim(
        jnp.zeros((text,), F32), gain_context, b * tcol, 0
    )
    grad_res_gains = sum_small(
        jnp.concatenate([gain_context_full, gain_latent, gain_post, gain_final])
    ).reshape(4, text)

    dfc2_low = dvision_out.astype(BF)
    bias_two = jnp.sum(dfc2_low.astype(F32), axis=0)
    (dfc1_pre,) = gelu_pull(dot(dfc2_low, fc2_full, 1, 0))
    dfc1_low = dfc1_pre.astype(BF)
    bias_fc1 = jnp.sum(dfc1_low.astype(F32), axis=0)
    dfc1_all = gather_blk_later(dfc1_low).reshape(tokens, -1)
    dnormed_two = sum_tp(dot(dfc1_low, fc1_full, 1, 1))
    dhidden_part, gain_two, shift_two = norm_two_pull(dnormed_two)
    dhidden_one = dvision_out + dhidden_part
    dattn_total = dhidden_one.astype(BF)
    bias_one = jnp.sum(dattn_total.astype(F32), axis=0)
    dattn_output = dot(dattn_total, out_full, 1, 0).astype(BF)

    dout_heads = dattn_output.reshape(tok, heads, HEAD_VIS)
    vis_delta = jnp.sum(dout_heads.astype(F32) * vis_result, axis=-1)
    d_high, d_low = halves(vis_delta)
    l_high, l_low = halves(vis_lse.T)
    dout_all = gather_blk(
        jnp.concatenate(
            [dattn_output, jnp.concatenate([d_high, d_low, l_high, l_low], axis=1).astype(BF)],
            axis=1,
        )
    ).reshape(tokens, -1)
    width = heads * HEAD_VIS
    row_values = dout_all[:, width:].astype(F32).reshape(tokens, 2, 2, heads).sum(axis=2)
    delta_all, lse_all = row_values[:, 0].T, row_values[:, 1].T
    dout_all_heads = dout_all[:, :width].reshape(tokens, heads, HEAD_VIS)
    prob = jnp.exp(scores - vis_lse[..., None])
    dprob_vis = mm("qhd,khd->hqk", dout_heads, value_all)
    dscores_vis = (prob * (dprob_vis - vis_delta.T[..., None])).astype(BF)
    dquery_home = mm("hqk,khd->qhd", dscores_vis, key_all) * vis_scale
    scores_in = mm("khd,qhd->hkq", key_heads, query_all) * vis_scale
    scores_in = jnp.where(allowed_vis[None], scores_in, -jnp.inf)
    prob_in = jnp.exp(scores_in - lse_all[:, None, :])
    dprob_in = mm("khd,qhd->hkq", value_heads, dout_all_heads)
    dscores_in = (prob_in * (dprob_in - delta_all[:, None, :])).astype(BF)
    dkey_home = mm("hkq,qhd->khd", dscores_in, query_all) * vis_scale
    dvalue_home = mm("hkq,qhd->khd", prob_in.astype(BF), dout_all_heads)
    dqkv_low = jnp.stack(
        [
            dquery_home.reshape(tok, -1),
            dkey_home.reshape(tok, -1),
            dvalue_home.reshape(tok, -1),
        ]
    ).astype(BF)
    bias_qv = jnp.stack(
        [jnp.sum(dqkv_low[0].astype(F32), axis=0), jnp.sum(dqkv_low[2].astype(F32), axis=0)]
    )
    dqkv_all = gather_blk(dqkv_low)
    dnormed_one = sum_tp(
        dot(dqkv_low[0], qkv_full[0], 1, 1)
        + dot(dqkv_low[1], qkv_full[1], 1, 1)
        + dot(dqkv_low[2], qkv_full[2], 1, 1)
    )
    dinput_part, gain_one, shift_one = norm_one_pull(dnormed_one)
    patches_grad = dhidden_one + dinput_part

    dcols = exchange(
        jnp.stack([dfc2_low, dattn_total]).reshape(2, tok, blk, wcol).transpose(2, 0, 1, 3), "blk"
    )
    dfc2_cols = dcols[:, 0].reshape(tokens, wcol)
    dattn_vis_cols = dcols[:, 1].reshape(tokens, wcol)
    grad_vis_fc2 = dot(dfc2_cols, fc1_low_all, 0, 0).T
    grad_vis_out = dot(dattn_vis_cols, attn_out_all, 0, 0).T
    grad_vis_fc1 = dot(mlp_cols, dfc1_all, 0, 0)
    grad_vis_qkv = jnp.stack(
        [
            dot(attn_cols, dqkv_all[:, j].reshape(tokens, -1), 0, 0)
            for j in range(3)
        ],
        axis=1,
    )
    small = jnp.concatenate(
        [
            gain_one,
            gain_two,
            shift_one,
            shift_two,
            bias_one,
            bias_two,
            bias_qv.reshape(-1),
            bias_fc1,
        ]
    )
    small = jnp.sum(gather_blk(small), axis=0)
    grad_vis_gains = small[: 2 * wide].reshape(2, wide)
    grad_vis_shifts = small[2 * wide : 4 * wide].reshape(2, wide)
    grad_vis_out_bias = small[4 * wide : 6 * wide].reshape(2, wide)
    grad_vis_qv_bias = small[6 * wide : 6 * wide + 2 * width].reshape(2, width)
    grad_vis_fc1_bias = small[6 * wide + 2 * width :]
    return (
        latents_out,
        patches_grad,
        latents_grad,
        grad_vis_gains,
        grad_vis_shifts,
        grad_vis_qkv,
        grad_vis_qv_bias,
        grad_vis_out,
        grad_vis_out_bias,
        grad_vis_fc1,
        grad_vis_fc1_bias,
        grad_vis_fc2,
        grad_proj_gate_up,
        grad_proj_down,
        grad_res_gains,
        grad_res_q,
        grad_res_kv,
        grad_res_out,
        grad_res_gate_up,
        grad_res_down,
    )


def solution(mesh):
    placed = (
        P("blk", None),
        P("blk", None),
        P(),
        P(),
        P(),
        P(),
        P("blk", None, "tp"),
        P(None, "tp"),
        P("tp", "blk"),
        P(),
        P("blk", "tp"),
        P("tp"),
        P("tp", "blk"),
        P("blk", None, "tp"),
        P("tp", "blk"),
        P(),
        P("blk", "tp"),
        P("blk", None, "tp"),
        P("tp", "blk"),
        P(None, None, ("blk", "tp")),
        P(("blk", "tp"), None),
        P("blk", None),
    )
    return jax.shard_map(
        per_device,
        mesh=mesh,
        in_specs=placed,
        out_specs=(
            P("blk", None),
            P("blk", None),
            P("blk", None),
            P(),
            P(),
            P("blk", None, "tp"),
            P(None, "tp"),
            P("tp", "blk"),
            P(),
            P("blk", "tp"),
            P("tp"),
            P("tp", "blk"),
            P("blk", None, "tp"),
            P("tp", "blk"),
            P(),
            P("blk", "tp"),
            P("blk", None, "tp"),
            P("tp", "blk"),
            P(None, None, ("blk", "tp")),
            P(("blk", "tp"), None),
        ),
        check_vma=False,
    )
```

```python
import jax
import jax.numpy as jnp
from jax import lax
from jax.experimental import pallas as pl
from jax.experimental.layout import Layout, with_layout_constraint
from jax.experimental.pallas import tpu as pltpu
from jax.sharding import PartitionSpec as P

HEADS = 16
HEAD_VIS = 72
RES_HEAD = 96
LATENTS = 64
EPSILON = 1e-06
EVERY = ("blk", "tp")
BF = jnp.bfloat16
F32 = jnp.float32


def swap_core(value):
    return lax.ppermute(value, "tp", [(i, i ^ 1) for i in range(lax.axis_size("tp"))])


def swap_x(value):
    return lax.ppermute(value, "tp", [(i, i ^ 2) for i in range(lax.axis_size("tp"))])


def my_x():
    return lax.axis_index("tp") // 2


def my_core():
    return lax.axis_index("tp") % 2


def pick(flag, one, zero):
    return jnp.where(flag == 1, one, zero)


def exchange(chunks, axis):
    return lax.all_to_all(chunks, axis, 0, 0, tiled=True)


def gather_direct(value, axis, count):
    return exchange(jnp.broadcast_to(value[None], (count,) + value.shape), axis)


def sum_blk(partial):
    return jnp.sum(exchange(partial.astype(BF), "blk").astype(F32), axis=0)


def sum_tp_quarter(partial):
    pairs = partial.reshape((2, 2) + partial.shape[1:])
    core, x = my_core(), my_x()
    keep = pick(core, pairs[:, 1], pairs[:, 0])
    send = pick(core, pairs[:, 0], pairs[:, 1]).astype(BF)
    half = keep + swap_core(send).astype(F32)
    keep = pick(x, half[1], half[0])
    send = pick(x, half[0], half[1]).astype(BF)
    return keep + swap_x(send).astype(F32)


def gather_tp(value):
    other = swap_x(value)
    x, core = my_x(), my_core()
    both = pick(x, jnp.stack([other, value]), jnp.stack([value, other]))
    far = swap_core(both)
    quad = pick(core, jnp.stack([far, both], axis=1), jnp.stack([both, far], axis=1))
    return quad.reshape((4,) + value.shape)


def sum_tp(partial):
    chip = (partial + swap_core(partial)).astype(BF)
    return chip.astype(F32) + swap_x(chip).astype(F32)


def gather_blk(value):
    return gather_direct(value, "blk", lax.axis_size("blk"))


def gather_blk_later(value):
    return lax.all_gather(value, "blk", axis=0, tiled=False)


def gather_every(value):
    return gather_tp(gather_blk(value))


def sum_every(partial):
    return sum_blk(sum_tp_quarter(partial))


def ring_order():
    count = lax.axis_size("blk")
    return list(range(0, count, 2)) + list(range(count - 1, 0, -2))


def ring_index(distance):
    order = ring_order()
    count = len(order)
    after = [order[(order.index(i) + distance) % count] for i in range(count)]
    return jnp.array(after, jnp.int32)[lax.axis_index("blk")]


def pass_on(value, step):
    order = ring_order()
    count = len(order)
    route = [(order[i], order[(i + step) % count]) for i in range(count)]
    return lax.ppermute(value, "blk", route)


def ring_gather(own):
    count = lax.axis_size("blk")
    half, rows = count // 2, own.shape[0] // 2
    blocks = [own] + [None] * (count - 1)
    ahead = behind = own
    for k in range(1, half):
        behind = pass_on(behind, 1)
        ahead = pass_on(ahead, -1)
        blocks[count - k], blocks[k] = behind, ahead
    blocks[half] = jnp.concatenate(
        [pass_on(behind[:rows], 1), pass_on(ahead[rows:], -1)], axis=0
    )
    return blocks


def ring_sum(part):
    count = lax.axis_size("blk")
    half = count // 2
    far = part(half)
    rows = far.shape[0] // 2
    low = far.astype(BF)
    onward, back = pass_on(low[:rows], 1), pass_on(low[rows:], -1)
    for k in range(half - 1, 0, -1):
        one, two = part(k), part(count - k)
        if k == half - 1:
            blank = jnp.zeros_like(onward)
            onward = jnp.concatenate([onward, blank], axis=0)
            back = jnp.concatenate([blank, back], axis=0)
        onward = pass_on((one + onward.astype(F32)).astype(BF), 1)
        back = pass_on((two + back.astype(F32)).astype(BF), -1)
    return part(0) + onward.astype(F32) + back.astype(F32)


def place_blocks(blocks):
    count = len(blocks)
    places = jnp.stack([ring_index(k) for k in range(count)])

    def kernel(places_ref, *refs):
        for k in range(count):
            refs[count][places_ref[k]] = refs[k][...]

    return pl.pallas_call(
        kernel,
        out_shape=jax.ShapeDtypeStruct((count,) + blocks[0].shape, blocks[0].dtype),
        in_specs=[pl.BlockSpec(memory_space=pltpu.SMEM)]
        + [pl.BlockSpec(memory_space=pltpu.VMEM)] * count,
        out_specs=pl.BlockSpec(memory_space=pltpu.VMEM),
        compiler_params=pltpu.CompilerParams(vmem_limit_bytes=24 * 2**20),
        name="place_blocks",
    )(places, *blocks)


def after(value, *others):
    return lax.optimization_barrier((value,) + others)[0]


def ring_groups():
    count = lax.axis_size("blk")
    half = count // 2
    return [[0]] + [[k, count - k] for k in range(1, half)] + [[half]]


def gather_rows_every(own):
    blocks = ring_gather(own)
    parts = []
    for group in ring_groups():
        parts.append(gather_tp(jnp.concatenate([blocks[k] for k in group], axis=0)))
    return jnp.concatenate([part.reshape((-1,) + own.shape[1:]) for part in parts], axis=0)


def sum_rows_every(partial, rows):
    start, sums = 0, {}
    pieces = []
    for group in ring_groups():
        size = 4 * len(group) * rows
        pieces.append((group, partial[start : start + size]))
        start += size
    for group, piece in reversed(pieces):
        total = sum_tp_quarter(piece.reshape((4, len(group) * rows) + partial.shape[1:]))
        for place, k in enumerate(group):
            sums[k] = total[place * rows : (place + 1) * rows]
    return ring_sum(lambda k: sums[k])


def layer_norm(values, gain, shift):
    center = values - jnp.mean(values, axis=-1, keepdims=True)
    spread = jnp.mean(center * center, axis=-1, keepdims=True)
    return center * lax.rsqrt(spread + EPSILON) * gain + shift


def rms_norm(values, gain):
    return values * lax.rsqrt(jnp.mean(values * values, axis=-1, keepdims=True) + EPSILON) * gain


def gelu_tanh(values):
    return jax.nn.gelu(values, approximate=True)


def swiglu(gate_part, up_part):
    return jax.nn.silu(gate_part) * up_part


def mm(spec, left, right):
    return jnp.einsum(spec, left, right, preferred_element_type=F32)


def dot(left, right, on_left, on_right):
    return lax.dot_general(
        left, right, (((on_left,), (on_right,)), ((), ())), preferred_element_type=F32
    )


def halves(value):
    high = lax.reduce_precision(value, 8, 7)
    return high, lax.reduce_precision(value - high, 8, 7)


def stream_images(image_patches, span_order, tok_rows):
    bounds = jnp.cumsum(image_patches)
    rows = span_order[:, None] * tok_rows + jnp.arange(tok_rows, dtype=jnp.int32)[None, :]
    stream = rows.reshape(-1)
    return jnp.sum((stream[:, None] >= bounds[None, :]).astype(jnp.int32), axis=1)


def per_device(
    patches,
    latents,
    image_patches,
    span_order,
    vis_gains,
    vis_shifts,
    vis_qkv,
    vis_qv_bias,
    vis_out,
    vis_out_bias,
    vis_fc1,
    vis_fc1_bias,
    vis_fc2,
    proj_gate_up,
    proj_down,
    res_gains,
    res_q,
    res_kv,
    res_out,
    res_gate_up,
    res_down,
    out_grad,
):
    blk = lax.axis_size("blk")
    b, t = lax.axis_index("blk"), lax.axis_index("tp")
    tok, wide = patches.shape
    lat, text = latents.shape
    sub, lsub = tok // 4, lat // 4
    tokens, lats = tok * blk, lat * blk
    wcol, tcol = wide // blk, text // blk
    heads = HEADS // 4
    unit = proj_down.shape[0] // blk
    hidden = proj_down.shape[0]
    qcols = res_q.shape[1]
    kvcols = RES_HEAD

    attn_shard = jnp.concatenate([vis_qkv.transpose(1, 0, 2), vis_out.T[None]], axis=0)
    attn_ring = ring_gather(attn_shard)
    attn_full = place_blocks(attn_ring)
    attn_full = attn_full.transpose(1, 0, 2, 3).reshape(4, wide, -1)
    qkv_full, out_full = attn_full[:3], attn_full[3]
    gu_chunks = proj_gate_up.reshape(wcol, 2, blk, unit).transpose(2, 1, 0, 3)
    fc1_ring = ring_gather(after(vis_fc1, attn_ring[blk // 2]))
    fc1_full = place_blocks(fc1_ring).reshape(wide, -1)
    fc2_full = gather_blk_later(vis_fc2.T).reshape(wide, -1)
    rkv_own = res_kv.reshape(tcol, 2 * kvcols)
    rkv_quad = gather_tp(rkv_own)

    latent_in = latents.astype(F32)
    latent_low = rms_norm(latent_in, res_gains[1]).astype(BF)
    all_images = stream_images(image_patches, span_order, tok)
    own_images = lax.dynamic_slice_in_dim(all_images, b * tok, tok)
    allowed_vis = own_images[:, None] == all_images[None, :]
    inputs = patches.astype(F32)
    normed_one, norm_one_pull = jax.vjp(layer_norm, inputs, vis_gains[0], vis_shifts[0])
    attn_input = normed_one.astype(BF)
    query_rows = (dot(attn_input, qkv_full[0], 1, 0) + vis_qv_bias[0]).astype(BF)
    key_rows = dot(attn_input, qkv_full[1], 1, 0).astype(BF)
    value_rows = (dot(attn_input, qkv_full[2], 1, 0) + vis_qv_bias[1]).astype(BF)
    kv_all = jnp.stack(ring_gather(jnp.concatenate([key_rows, value_rows], axis=1)))
    rout_full = gather_blk_later(after(res_out.T, attn_ring[blk // 2])).reshape(text, -1)
    key_all = kv_all[:, :, : heads * HEAD_VIS].reshape(tokens, heads, HEAD_VIS)
    value_all = kv_all[:, :, heads * HEAD_VIS :].reshape(tokens, heads, HEAD_VIS)
    ring_images = jnp.stack(
        [all_images.reshape(blk, tok)[ring_index(k)] for k in range(blk)]
    ).reshape(-1)
    allowed_ring = own_images[:, None] == ring_images[None, :]
    query_heads = query_rows.reshape(tok, heads, HEAD_VIS)
    key_heads = key_rows.reshape(tok, heads, HEAD_VIS)
    value_heads = value_rows.reshape(tok, heads, HEAD_VIS)
    vis_scale = HEAD_VIS ** (-0.5)
    scores = mm("qhd,khd->hqk", query_heads, key_all) * vis_scale
    scores = jnp.where(allowed_ring[None], scores, -jnp.inf)
    row_top = jnp.max(scores, axis=-1)
    weights = jnp.exp(scores - row_top[..., None])
    weight_sum = jnp.sum(weights, axis=-1)
    weighted = mm("hqk,khd->hqd", weights.astype(BF), value_all)
    vis_lse = row_top + jnp.log(weight_sum)
    vis_result = (weighted / weight_sum[..., None]).transpose(1, 0, 2)
    attn_output = vis_result.astype(BF).reshape(tok, -1)

    gate_own = exchange(after(gu_chunks[:, 0], kv_all), "blk").reshape(wide, unit)
    up_own = exchange(after(gu_chunks[:, 1], gate_own), "blk").reshape(wide, unit)

    hidden_one = inputs + sum_tp(dot(attn_output, out_full, 1, 1)) + vis_out_bias[0]
    hidden_one, gate_own = lax.optimization_barrier((hidden_one, gate_own))
    normed_two, norm_two_pull = jax.vjp(layer_norm, hidden_one, vis_gains[1], vis_shifts[1])
    mlp_input = normed_two.astype(BF)
    fc1_pre = dot(mlp_input, fc1_full, 1, 0) + vis_fc1_bias
    fc1_act, gelu_pull = jax.vjp(gelu_tanh, fc1_pre)
    fc1_low = fc1_act.astype(BF)
    fc2_part = dot(fc1_low, fc2_full, 1, 1).reshape(4, sub, wide)
    hidden_sub = lax.dynamic_slice_in_dim(hidden_one, t * sub, sub)
    vision_sub = hidden_sub + sum_tp_quarter(fc2_part) + vis_out_bias[1]
    vision_sub, up_own, rout_full = lax.optimization_barrier((vision_sub, up_own, rout_full))
    vision_low = gather_every(vision_sub.astype(BF)).reshape(tokens, wide)

    latent_low = after(latent_low, hidden_one)
    latent_cols = exchange(latent_low.reshape(lat, blk, tcol).transpose(1, 0, 2), "blk")
    latent_cols = latent_cols.reshape(lats, tcol)
    latent_qkv = sum_blk(
        jnp.concatenate([dot(latent_cols, res_q, 1, 0), dot(latent_cols, rkv_own, 1, 0)], axis=1)
        .astype(BF)
        .reshape(blk, lat, qcols + 2 * kvcols)
    ).astype(BF)

    vision_low, latent_qkv = lax.optimization_barrier((vision_low, latent_qkv))
    latent_query = latent_qkv[:, :qcols]
    latent_kv = latent_qkv[:, qcols:]

    gate = dot(vision_low, gate_own, 1, 0)
    up = dot(vision_low, up_own, 1, 0)
    proj_hidden, proj_pull = jax.vjp(swiglu, gate, up)
    proj_ring = ring_gather(proj_hidden.astype(BF))
    pdown = proj_down.reshape(blk, unit, tcol)
    pdown_ring = [lax.dynamic_index_in_dim(pdown, ring_index(k), 0, False) for k in range(blk)]
    context_part = dot(proj_ring[0], pdown_ring[0], 1, 0)
    for k in sorted(range(1, blk), key=lambda k: min(k, blk - k)):
        context_part = context_part + dot(proj_ring[k], pdown_ring[k], 1, 0)
    kept = jnp.concatenate([query_rows, attn_output, fc1_low], axis=1)
    kept_all = gather_blk_later(after(kept, context_part)).reshape(tokens, -1)
    quarter = tokens // 4
    context = sum_tp_quarter(context_part.reshape(4, quarter, tcol))
    gain_latent_own = lax.dynamic_slice_in_dim(res_gains[1], b * tcol, tcol)
    gain_context_own = lax.dynamic_slice_in_dim(res_gains[0], b * tcol, tcol)
    scaled_low = (context * gain_context_own).astype(BF)
    kv_part = mm("kc,tcj->tkj", scaled_low, rkv_quad)
    square_part = jnp.sum(context * context, axis=-1)
    high, low = halves(square_part)
    stats = jnp.pad(jnp.stack([high, low], axis=1), ((0, 0), (0, 2 * kvcols - 2)))
    kv_sums = sum_blk(
        jnp.concatenate([kv_part, stats[None]], axis=0)
        .astype(BF)
        .reshape(5, blk, sub, 2 * kvcols)
        .transpose(1, 0, 2, 3)
    )
    scale_sub = lax.rsqrt((kv_sums[4, :, 0] + kv_sums[4, :, 1]) / text + EPSILON)
    patch_kv = (kv_sums[:4] * scale_sub[None, :, None]).astype(BF)
    patch_all = exchange(
        jnp.broadcast_to(patch_kv[None], (blk,) + patch_kv.shape).reshape(4 * blk, sub, -1), EVERY
    ).reshape(tokens, 2 * kvcols)

    latent_images = b * (lat // LATENTS) + jnp.arange(lat, dtype=jnp.int32) // LATENTS
    key_images = jnp.concatenate([all_images, latent_images])
    allowed_res = latent_images[:, None] == key_images[None, :]
    res_kv_all = jnp.concatenate([patch_all, latent_kv], axis=0)
    res_key, res_value = res_kv_all[:, :kvcols], res_kv_all[:, kvcols:]
    group = qcols // RES_HEAD
    res_query = latent_query.reshape(lat, group, RES_HEAD)
    res_scale = RES_HEAD ** (-0.5)
    res_scores = mm("qgd,nd->gqn", res_query, res_key) * res_scale
    res_scores = jnp.where(allowed_res[None], res_scores, -jnp.inf)
    res_top = jnp.max(res_scores, axis=-1)
    res_weights = jnp.exp(res_scores - res_top[..., None])
    res_sum = jnp.sum(res_weights, axis=-1)
    res_result = (
        mm("gqn,nd->gqd", res_weights.astype(BF), res_value) / res_sum[..., None]
    ).transpose(1, 0, 2)
    res_lse = res_top + jnp.log(res_sum)
    result_low = res_result.astype(BF).reshape(lat, qcols)

    latent_sub = lax.dynamic_slice_in_dim(latent_in, t * lsub, lsub)
    latent_one = latent_sub + sum_tp_quarter(
        dot(result_low, rout_full, 1, 1).reshape(4, lsub, text)
    )
    post_normed, post_pull = jax.vjp(rms_norm, latent_one, res_gains[2])
    post_all = gather_rows_every(post_normed.astype(BF))
    gate_up_two = mm("td,dje->tje", post_all, res_gate_up)
    mlp_hidden, mlp_pull = jax.vjp(swiglu, gate_up_two[:, 0], gate_up_two[:, 1])
    mlp_low = mlp_hidden.astype(BF)
    latent_two = latent_one + sum_rows_every(dot(mlp_low, res_down, 1, 0), lsub)
    latent_two, kept_all = lax.optimization_barrier((latent_two, kept_all))
    width = heads * HEAD_VIS
    query_all = kept_all[:, :width].reshape(tokens, heads, HEAD_VIS)
    attn_out_all = kept_all[:, width : 2 * width]
    fc1_low_all = kept_all[:, 2 * width :]
    final_normed, final_pull = jax.vjp(rms_norm, latent_two, res_gains[3])
    grad_sub = lax.dynamic_slice_in_dim(out_grad, t * lsub, lsub).astype(F32)
    dlatent_two, gain_final = final_pull(grad_sub)
    latents_out = gather_tp(final_normed).reshape(lat, text)

    dmlp_all = gather_rows_every(dlatent_two.astype(BF))
    dgate_two, dup_two = mlp_pull(dot(dmlp_all, res_down, 1, 1))
    dgate_up_two = jnp.stack([dgate_two, dup_two], axis=1).astype(BF)
    dpost = sum_rows_every(mm("tje,dje->td", dgate_up_two, res_gate_up), lsub)
    dlatent_part, gain_post = post_pull(dpost)
    dlatent_one = dlatent_two + dlatent_part
    dattn_low = gather_tp(dlatent_one.astype(BF)).reshape(lat, text)
    gain_rows = jnp.stack([gain_post, gain_final]).reshape(2, 4, -1).transpose(1, 0, 2)
    gain_rows = sum_tp_quarter(gain_rows)

    dresult = dot(dattn_low, rout_full, 1, 0).astype(BF)
    dresult_heads = dresult.reshape(lat, group, RES_HEAD)
    res_delta = jnp.sum(dresult_heads.astype(F32) * res_result, axis=-1).T
    res_prob = jnp.exp(res_scores - res_lse[..., None])
    dprob = mm("qgd,nd->gqn", dresult_heads, res_value)
    dscores = (res_prob * (dprob - res_delta[..., None])).astype(BF)
    dquery = mm("gqn,nd->qgd", dscores, res_key) * res_scale
    dkey = mm("gqn,qgd->nd", dscores, res_query) * res_scale
    dvalue = mm("gqn,qgd->nd", res_prob.astype(BF), dresult_heads)
    dquery_own = dquery.reshape(lat, qcols).astype(BF)
    dkv_low = jnp.concatenate([dkey, dvalue], axis=1).astype(BF)
    dpatch_local, dlatent_kv = dkv_low[:tokens], dkv_low[tokens:]
    dpatch_sub = jnp.sum(
        exchange(dpatch_local.reshape(4 * blk, sub, 2 * kvcols), EVERY)
        .reshape(blk, 4, sub, 2 * kvcols)
        .astype(F32),
        axis=0,
    )
    along = jnp.sum(dpatch_sub * patch_kv.astype(F32), axis=(0, 2)) / text
    a_high, a_low = halves(along)
    s_high, s_low = halves(scale_sub)
    row_stats = jnp.pad(
        jnp.stack([a_high, a_low, s_high, s_low], axis=1), ((0, 0), (0, 2 * kvcols - 4))
    )
    dpatch_rows = gather_blk(jnp.concatenate([dpatch_sub, row_stats[None]], axis=0).astype(BF))
    dpatch_rows = dpatch_rows.transpose(1, 0, 2, 3).reshape(5, quarter, 2 * kvcols)
    dpatch_quad = dpatch_rows[:4]
    along_rows = dpatch_rows[4, :, 0].astype(F32) + dpatch_rows[4, :, 1].astype(F32)
    scale_rows = dpatch_rows[4, :, 2].astype(F32) + dpatch_rows[4, :, 3].astype(F32)
    dcontext_normed = mm("tkj,tcj->kc", dpatch_quad, rkv_quad)
    unit_context = context * scale_rows[:, None]
    dcontext = scale_rows[:, None] * (
        dcontext_normed * gain_context_own - unit_context * along_rows[:, None]
    )
    gain_context = jnp.sum(dcontext_normed * unit_context, axis=0)
    context_low = (unit_context * gain_context_own).astype(BF)

    dcontext_low = gather_tp(dcontext.astype(BF)).reshape(tokens, tcol)
    dproj = ring_sum(lambda k: dot(dcontext_low, pdown_ring[k], 1, 1))
    mlp_late, post_late = after(mlp_low, dcontext_low), after(post_all, dcontext_low)
    grad_res_down = dot(mlp_late, dmlp_all, 0, 0)
    grad_res_gate_up = mm("td,tje->dje", post_late, dgate_up_two)
    grad_proj_down = jnp.zeros((blk, unit, tcol), F32)
    for k in range(blk):
        grad_proj_down = lax.dynamic_update_index_in_dim(
            grad_proj_down, dot(proj_ring[k], dcontext_low, 0, 0), ring_index(k), 0
        )
    grad_proj_down = grad_proj_down.reshape(hidden, tcol)
    res_rows = jnp.concatenate([dquery_own, dlatent_kv, result_low], axis=1)
    res_rows = gather_blk(after(res_rows, dcontext_low))
    res_rows = res_rows.reshape(lats, -1)
    dquery_all, dlkv_all = res_rows[:, :qcols], res_rows[:, qcols : qcols + 2 * kvcols]
    result_all = res_rows[:, qcols + 2 * kvcols :]
    grad_res_q = dot(latent_cols, dquery_all, 0, 0)
    grad_res_kv = dot(latent_cols, dlkv_all, 0, 0) + sum_tp_quarter(
        mm("kc,tkj->tcj", context_low, dpatch_quad)
    )
    grad_res_kv = grad_res_kv.reshape(tcol, 2, kvcols)
    dlatent_part = dot(dquery_all, res_q, 1, 1) + dot(dlkv_all, rkv_own, 1, 1)
    gain_latent = jnp.sum(dlatent_part * latent_cols.astype(F32), axis=0) / gain_latent_own
    dlatent_rows = exchange(dlatent_part.astype(BF).reshape(4 * blk, lsub, tcol), EVERY)
    dlatent_normed = (
        jnp.sum(dlatent_rows.reshape(blk, 4, lsub, tcol).astype(F32), axis=1)
        .transpose(1, 0, 2)
        .reshape(lsub, text)
    )
    latent_pull = jax.vjp(rms_norm, latent_sub, res_gains[1])[1]
    dlatent_in, _ = latent_pull(dlatent_normed)
    latents_grad = gather_tp(dlatent_one + dlatent_in).reshape(lat, text)
    dattn_cols = exchange(dattn_low.reshape(lat, blk, tcol).transpose(1, 0, 2), "blk")
    grad_res_out = dot(result_all, dattn_cols.reshape(lats, tcol), 0, 0)
    gain_cols = sum_tp(jnp.stack([gain_context, gain_latent]))
    dproj, grad_res_down, grad_res_gate_up, grad_proj_down, latents_grad, grad_res_out = (
        lax.optimization_barrier(
            (dproj, grad_res_down, grad_res_gate_up, grad_proj_down, latents_grad, grad_res_out)
        )
    )
    dgate, dup = proj_pull(dproj)
    dgate_low, dup_low = dgate.astype(BF), dup.astype(BF)
    dvision_part = dot(dgate_low, gate_own, 1, 1) + dot(dup_low, up_own, 1, 1)
    dvision_sub = sum_every(dvision_part.reshape(4, blk, sub, wide))
    dvision_out = gather_tp(dvision_sub).reshape(tok, wide)
    vision_late = after(vision_low, dvision_sub)
    grad_gu = jnp.stack([dot(vision_late, dgate_low, 0, 0), dot(vision_late, dup_low, 0, 0)])
    grad_gu = exchange(grad_gu.astype(BF).reshape(2, blk, wcol, unit).transpose(1, 0, 2, 3), "blk")

    dfc2_low = dvision_out.astype(BF)
    bias_two = jnp.sum(dfc2_low.astype(F32), axis=0)
    (dfc1_pre,) = gelu_pull(dot(dfc2_low, fc2_full, 1, 0))
    dfc1_low = dfc1_pre.astype(BF)
    bias_fc1 = jnp.sum(dfc1_low.astype(F32), axis=0)
    dfc1_all = gather_blk_later(dfc1_low).reshape(tokens, -1)
    dnormed_two = sum_tp(dot(dfc1_low, fc1_full, 1, 1))
    dhidden_part, gain_two, shift_two = norm_two_pull(dnormed_two)
    dhidden_one = dvision_out + dhidden_part
    dattn_total = dhidden_one.astype(BF)
    bias_one = jnp.sum(dattn_total.astype(F32), axis=0)
    dattn_output = dot(dattn_total, out_full, 1, 0).astype(BF)
    grad_res_gate_up = with_layout_constraint(
        grad_res_gate_up, Layout(major_to_minor=(0, 1, 2))
    )
    dattn_output, grad_gu, grad_res_gate_up = lax.optimization_barrier(
        (dattn_output, grad_gu, grad_res_gate_up)
    )
    grad_proj_gate_up = grad_gu.transpose(2, 1, 0, 3).reshape(wcol, 2, hidden).astype(F32)
    cols = after(jnp.stack([attn_input, mlp_input, dfc2_low, dattn_total]), dattn_output)
    cols = exchange(cols.reshape(4, tok, blk, wcol).transpose(2, 0, 1, 3), "blk")

    dout_heads = dattn_output.reshape(tok, heads, HEAD_VIS)
    vis_delta = jnp.sum(dout_heads.astype(F32) * vis_result, axis=-1)
    d_high, d_low = halves(vis_delta)
    l_high, l_low = halves(vis_lse.T)
    dout_all = gather_blk(
        jnp.concatenate(
            [dattn_output, jnp.concatenate([d_high, d_low, l_high, l_low], axis=1).astype(BF)],
            axis=1,
        )
    ).reshape(tokens, -1)
    row_values = dout_all[:, width:].astype(F32).reshape(tokens, 2, 2, heads).sum(axis=2)
    delta_all, lse_all = row_values[:, 0].T, row_values[:, 1].T
    dout_all_heads = dout_all[:, :width].reshape(tokens, heads, HEAD_VIS)
    prob = jnp.exp(scores - vis_lse[..., None])
    dprob_vis = mm("qhd,khd->hqk", dout_heads, value_all)
    dscores_vis = (prob * (dprob_vis - vis_delta.T[..., None])).astype(BF)
    dquery_home = mm("hqk,khd->qhd", dscores_vis, key_all) * vis_scale
    scores_in = mm("khd,qhd->hkq", key_heads, query_all) * vis_scale
    scores_in = jnp.where(allowed_vis[None], scores_in, -jnp.inf)
    prob_in = jnp.exp(scores_in - lse_all[:, None, :])
    dprob_in = mm("khd,qhd->hkq", value_heads, dout_all_heads)
    dscores_in = (prob_in * (dprob_in - delta_all[:, None, :])).astype(BF)
    dkey_home = mm("hkq,qhd->khd", dscores_in, query_all) * vis_scale
    dvalue_home = mm("hkq,qhd->khd", prob_in.astype(BF), dout_all_heads)
    dqkv_low = jnp.stack(
        [
            dquery_home.reshape(tok, -1),
            dkey_home.reshape(tok, -1),
            dvalue_home.reshape(tok, -1),
        ]
    ).astype(BF)
    dqkv_low, cols = lax.optimization_barrier((dqkv_low, cols))
    bias_qv = jnp.stack(
        [jnp.sum(dqkv_low[0].astype(F32), axis=0), jnp.sum(dqkv_low[2].astype(F32), axis=0)]
    )
    attn_cols, mlp_cols, dfc2_cols, dattn_vis_cols = (
        cols[:, j].reshape(tokens, wcol) for j in range(4)
    )
    dqkv_ring = ring_gather(jnp.concatenate(list(dqkv_low), axis=1))
    dqkv_ring = jnp.concatenate(dqkv_ring, axis=0)
    attn_cols_ring = jnp.concatenate(
        [lax.dynamic_slice_in_dim(attn_cols, ring_index(k) * tok, tok) for k in range(blk)]
    )
    dnormed_one = sum_tp(
        dot(dqkv_low[0], qkv_full[0], 1, 1)
        + dot(dqkv_low[1], qkv_full[1], 1, 1)
        + dot(dqkv_low[2], qkv_full[2], 1, 1)
    )
    dinput_part, gain_one, shift_one = norm_one_pull(dnormed_one)
    patches_grad = dhidden_one + dinput_part

    grad_vis_fc2 = dot(dfc2_cols, fc1_low_all, 0, 0).T
    grad_vis_out = dot(dattn_vis_cols, attn_out_all, 0, 0).T
    grad_vis_fc1 = dot(mlp_cols, dfc1_all, 0, 0)
    grad_vis_qkv = dot(attn_cols_ring, dqkv_ring, 0, 0).reshape(wcol, 3, -1)
    small = jnp.concatenate(
        [
            gain_one,
            gain_two,
            shift_one,
            shift_two,
            bias_one,
            bias_two,
            bias_qv.reshape(-1),
            bias_fc1,
            gain_rows.reshape(-1),
            gain_cols.reshape(-1),
        ]
    )
    small = gather_blk(small)
    gain_cols = small[:, small.shape[1] - 2 * tcol :].reshape(blk, 2, tcol)
    small = jnp.sum(small[:, : small.shape[1] - 2 * tcol], axis=0)
    gain_rows = gather_tp(small[small.shape[0] - text // 2 :].reshape(2, text // 4))
    gain_rows = gain_rows.transpose(1, 0, 2).reshape(2, text)
    grad_res_gains = jnp.concatenate([gain_cols.transpose(1, 0, 2).reshape(2, text), gain_rows])
    grad_vis_gains = small[: 2 * wide].reshape(2, wide)
    grad_vis_shifts = small[2 * wide : 4 * wide].reshape(2, wide)
    grad_vis_out_bias = small[4 * wide : 6 * wide].reshape(2, wide)
    grad_vis_qv_bias = small[6 * wide : 6 * wide + 2 * width].reshape(2, width)
    grad_vis_fc1_bias = small[6 * wide + 2 * width : 6 * wide + 2 * width + bias_fc1.shape[0]]
    return (
        latents_out,
        patches_grad,
        latents_grad,
        grad_vis_gains,
        grad_vis_shifts,
        grad_vis_qkv,
        grad_vis_qv_bias,
        grad_vis_out,
        grad_vis_out_bias,
        grad_vis_fc1,
        grad_vis_fc1_bias,
        grad_vis_fc2,
        grad_proj_gate_up,
        grad_proj_down,
        grad_res_gains,
        grad_res_q,
        grad_res_kv,
        grad_res_out,
        grad_res_gate_up,
        grad_res_down,
    )


def solution(mesh):
    placed = (
        P("blk", None),
        P("blk", None),
        P(),
        P(),
        P(),
        P(),
        P("blk", None, "tp"),
        P(None, "tp"),
        P("tp", "blk"),
        P(),
        P("blk", "tp"),
        P("tp"),
        P("tp", "blk"),
        P("blk", None, "tp"),
        P("tp", "blk"),
        P(),
        P("blk", "tp"),
        P("blk", None, "tp"),
        P("tp", "blk"),
        P(None, None, ("blk", "tp")),
        P(("blk", "tp"), None),
        P("blk", None),
    )
    return jax.shard_map(
        per_device,
        mesh=mesh,
        in_specs=placed,
        out_specs=(
            P("blk", None),
            P("blk", None),
            P("blk", None),
            P(),
            P(),
            P("blk", None, "tp"),
            P(None, "tp"),
            P("tp", "blk"),
            P(),
            P("blk", "tp"),
            P("tp"),
            P("tp", "blk"),
            P("blk", None, "tp"),
            P("tp", "blk"),
            P(),
            P("blk", "tp"),
            P("blk", None, "tp"),
            P("tp", "blk"),
            P(None, None, ("blk", "tp")),
            P(("blk", "tp"), None),
        ),
        check_vma=False,
    )
```

```python
import jax
import jax.numpy as jnp
from jax import lax
from jax.experimental import pallas as pl
from jax.experimental.layout import Layout, with_layout_constraint
from jax.experimental.pallas import tpu as pltpu
from jax.sharding import PartitionSpec as P

HEADS = 16
HEAD_VIS = 72
RES_HEAD = 96
LATENTS = 64
EPSILON = 1e-06
EVERY = ("blk", "tp")
BF = jnp.bfloat16
F32 = jnp.float32


def swap_core(value):
    return lax.ppermute(value, "tp", [(i, i ^ 1) for i in range(lax.axis_size("tp"))])


def swap_x(value):
    return lax.ppermute(value, "tp", [(i, i ^ 2) for i in range(lax.axis_size("tp"))])


def my_x():
    return lax.axis_index("tp") // 2


def my_core():
    return lax.axis_index("tp") % 2


def pick(flag, one, zero):
    return jnp.where(flag == 1, one, zero)


def exchange(chunks, axis):
    return lax.all_to_all(chunks, axis, 0, 0, tiled=True)


def gather_direct(value, axis, count):
    return exchange(jnp.broadcast_to(value[None], (count,) + value.shape), axis)


def sum_blk(partial):
    return jnp.sum(exchange(partial.astype(BF), "blk").astype(F32), axis=0)


def sum_tp_quarter(partial):
    pairs = partial.reshape((2, 2) + partial.shape[1:])
    core, x = my_core(), my_x()
    keep = pick(core, pairs[:, 1], pairs[:, 0])
    send = pick(core, pairs[:, 0], pairs[:, 1]).astype(BF)
    half = keep + swap_core(send).astype(F32)
    keep = pick(x, half[1], half[0])
    send = pick(x, half[0], half[1]).astype(BF)
    return keep + swap_x(send).astype(F32)


def gather_tp(value):
    other = swap_x(value)
    x, core = my_x(), my_core()
    both = pick(x, jnp.stack([other, value]), jnp.stack([value, other]))
    far = swap_core(both)
    quad = pick(core, jnp.stack([far, both], axis=1), jnp.stack([both, far], axis=1))
    return quad.reshape((4,) + value.shape)


def sum_tp(partial):
    chip = (partial + swap_core(partial)).astype(BF)
    return chip.astype(F32) + swap_x(chip).astype(F32)


def gather_blk(value):
    return gather_direct(value, "blk", lax.axis_size("blk"))


def gather_blk_later(value):
    return lax.all_gather(value, "blk", axis=0, tiled=False)


def gather_every(value):
    return gather_tp(gather_blk(value))


def sum_every(partial):
    return sum_blk(sum_tp_quarter(partial))


def ring_order():
    count = lax.axis_size("blk")
    return list(range(0, count, 2)) + list(range(count - 1, 0, -2))


def ring_index(distance):
    order = ring_order()
    count = len(order)
    after = [order[(order.index(i) + distance) % count] for i in range(count)]
    return jnp.array(after, jnp.int32)[lax.axis_index("blk")]


def pass_on(value, step):
    order = ring_order()
    count = len(order)
    route = [(order[i], order[(i + step) % count]) for i in range(count)]
    return lax.ppermute(value, "blk", route)


def ring_gather(own):
    count = lax.axis_size("blk")
    half, rows = count // 2, own.shape[0] // 2
    blocks = [own] + [None] * (count - 1)
    ahead = behind = own
    for k in range(1, half):
        behind = pass_on(behind, 1)
        ahead = pass_on(ahead, -1)
        blocks[count - k], blocks[k] = behind, ahead
    blocks[half] = jnp.concatenate(
        [pass_on(behind[:rows], 1), pass_on(ahead[rows:], -1)], axis=0
    )
    return blocks


def ring_sum(part, arrivals=None):
    count = lax.axis_size("blk")
    half = count // 2
    far = part(half)
    rows = far.shape[0] // 2
    low = far.astype(BF)
    onward, back = pass_on(low[:rows], 1), pass_on(low[rows:], -1)
    for k in range(half - 1, 0, -1):
        one, two = part(k), part(count - k)
        if k == half - 1:
            blank = jnp.zeros_like(onward)
            onward = jnp.concatenate([onward, blank], axis=0)
            back = jnp.concatenate([blank, back], axis=0)
        if arrivals is not None:
            arrivals.append(onward)
        onward = pass_on((one + onward.astype(F32)).astype(BF), 1)
        back = pass_on((two + back.astype(F32)).astype(BF), -1)
    return part(0) + onward.astype(F32) + back.astype(F32)


def place_blocks(blocks):
    count = len(blocks)
    places = jnp.stack([ring_index(k) for k in range(count)])

    def kernel(places_ref, *refs):
        for k in range(count):
            refs[count][places_ref[k]] = refs[k][...]

    return pl.pallas_call(
        kernel,
        out_shape=jax.ShapeDtypeStruct((count,) + blocks[0].shape, blocks[0].dtype),
        in_specs=[pl.BlockSpec(memory_space=pltpu.SMEM)]
        + [pl.BlockSpec(memory_space=pltpu.VMEM)] * count,
        out_specs=pl.BlockSpec(memory_space=pltpu.VMEM),
        compiler_params=pltpu.CompilerParams(vmem_limit_bytes=24 * 2**20),
        name="place_blocks",
    )(places, *blocks)


def share_columns(rows):
    parts, own, count, width = rows.shape
    got = gather_tp(exchange(rows.transpose(2, 0, 1, 3), "blk"))
    return got.transpose(2, 1, 0, 3, 4).reshape(parts, count * 4 * own, width)


def after(value, *others):
    return lax.optimization_barrier((value,) + others)[0]


def ring_groups():
    count = lax.axis_size("blk")
    half = count // 2
    return [[0]] + [[k, count - k] for k in range(1, half)] + [[half]]


def gather_rows_every(own):
    blocks = ring_gather(own)
    parts = []
    for group in ring_groups():
        parts.append(gather_tp(jnp.concatenate([blocks[k] for k in group], axis=0)))
    return jnp.concatenate([part.reshape((-1,) + own.shape[1:]) for part in parts], axis=0)


def sum_rows_every(partial, rows):
    start, sums = 0, {}
    pieces = []
    for group in ring_groups():
        size = 4 * len(group) * rows
        pieces.append((group, partial[start : start + size]))
        start += size
    for group, piece in reversed(pieces):
        total = sum_tp_quarter(piece.reshape((4, len(group) * rows) + partial.shape[1:]))
        for place, k in enumerate(group):
            sums[k] = total[place * rows : (place + 1) * rows]
    return ring_sum(lambda k: sums[k])


def layer_norm(values, gain, shift):
    center = values - jnp.mean(values, axis=-1, keepdims=True)
    spread = jnp.mean(center * center, axis=-1, keepdims=True)
    return center * lax.rsqrt(spread + EPSILON) * gain + shift


def rms_norm(values, gain):
    return values * lax.rsqrt(jnp.mean(values * values, axis=-1, keepdims=True) + EPSILON) * gain


def gelu_tanh(values):
    return jax.nn.gelu(values, approximate=True)


def swiglu(gate_part, up_part):
    return jax.nn.silu(gate_part) * up_part


def mm(spec, left, right):
    return jnp.einsum(spec, left, right, preferred_element_type=F32)


def dot(left, right, on_left, on_right):
    return lax.dot_general(
        left, right, (((on_left,), (on_right,)), ((), ())), preferred_element_type=F32
    )


def halves(value):
    high = lax.reduce_precision(value, 8, 7)
    return high, lax.reduce_precision(value - high, 8, 7)


def stream_images(image_patches, span_order, tok_rows):
    bounds = jnp.cumsum(image_patches)
    rows = span_order[:, None] * tok_rows + jnp.arange(tok_rows, dtype=jnp.int32)[None, :]
    stream = rows.reshape(-1)
    return jnp.sum((stream[:, None] >= bounds[None, :]).astype(jnp.int32), axis=1)


def per_device(
    patches,
    latents,
    image_patches,
    span_order,
    vis_gains,
    vis_shifts,
    vis_qkv,
    vis_qv_bias,
    vis_out,
    vis_out_bias,
    vis_fc1,
    vis_fc1_bias,
    vis_fc2,
    proj_gate_up,
    proj_down,
    res_gains,
    res_q,
    res_kv,
    res_out,
    res_gate_up,
    res_down,
    out_grad,
):
    blk = lax.axis_size("blk")
    b, t = lax.axis_index("blk"), lax.axis_index("tp")
    tok, wide = patches.shape
    lat, text = latents.shape
    sub, lsub = tok // 4, lat // 4
    tokens, lats = tok * blk, lat * blk
    wcol, tcol = wide // blk, text // blk
    heads = HEADS // 4
    unit = proj_down.shape[0] // blk
    hidden = proj_down.shape[0]
    qcols = res_q.shape[1]
    kvcols = RES_HEAD

    attn_shard = jnp.concatenate([vis_qkv.transpose(1, 0, 2), vis_out.T[None]], axis=0)
    attn_ring = ring_gather(attn_shard)
    attn_full = place_blocks(attn_ring)
    attn_full = attn_full.transpose(1, 0, 2, 3).reshape(4, wide, -1)
    qkv_full, out_full = attn_full[:3], attn_full[3]
    gu_chunks = proj_gate_up.reshape(wcol, 2, blk, unit).transpose(2, 1, 0, 3)
    fc1_full = gather_blk_later(vis_fc1).reshape(wide, -1)
    fc2_full = gather_blk_later(vis_fc2.T).reshape(wide, -1)
    rkv_own = res_kv.reshape(tcol, 2 * kvcols)
    rkv_quad = gather_tp(rkv_own)

    all_images = stream_images(image_patches, span_order, tok)
    own_images = lax.dynamic_slice_in_dim(all_images, b * tok, tok)
    allowed_vis = own_images[:, None] == all_images[None, :]
    inputs = patches.astype(F32)
    normed_one, norm_one_pull = jax.vjp(layer_norm, inputs, vis_gains[0], vis_shifts[0])
    attn_input = normed_one.astype(BF)
    query_rows = (dot(attn_input, qkv_full[0], 1, 0) + vis_qv_bias[0]).astype(BF)
    key_rows = dot(attn_input, qkv_full[1], 1, 0).astype(BF)
    value_rows = (dot(attn_input, qkv_full[2], 1, 0) + vis_qv_bias[1]).astype(BF)
    kv_all = jnp.stack(ring_gather(jnp.concatenate([key_rows, value_rows], axis=1)))
    key_all = kv_all[:, :, : heads * HEAD_VIS].reshape(tokens, heads, HEAD_VIS)
    value_all = kv_all[:, :, heads * HEAD_VIS :].reshape(tokens, heads, HEAD_VIS)
    ring_images = jnp.stack(
        [all_images.reshape(blk, tok)[ring_index(k)] for k in range(blk)]
    ).reshape(-1)
    allowed_ring = own_images[:, None] == ring_images[None, :]
    query_heads = query_rows.reshape(tok, heads, HEAD_VIS)
    key_heads = key_rows.reshape(tok, heads, HEAD_VIS)
    value_heads = value_rows.reshape(tok, heads, HEAD_VIS)
    vis_scale = HEAD_VIS ** (-0.5)
    scores = mm("qhd,khd->hqk", query_heads, key_all) * vis_scale
    scores = jnp.where(allowed_ring[None], scores, -jnp.inf)
    row_top = jnp.max(scores, axis=-1)
    weights = jnp.exp(scores - row_top[..., None])
    weight_sum = jnp.sum(weights, axis=-1)
    weighted = mm("hqk,khd->hqd", weights.astype(BF), value_all)
    vis_lse = row_top + jnp.log(weight_sum)
    vis_result = (weighted / weight_sum[..., None]).transpose(1, 0, 2)
    attn_output = vis_result.astype(BF).reshape(tok, -1)

    gate_own = exchange(after(gu_chunks[:, 0], kv_all), "blk").reshape(wide, unit)
    up_own = exchange(after(gu_chunks[:, 1], gate_own), "blk").reshape(wide, unit)

    hidden_one = inputs + sum_tp(dot(attn_output, out_full, 1, 1)) + vis_out_bias[0]
    hidden_one, gate_own = lax.optimization_barrier((hidden_one, gate_own))
    normed_two, norm_two_pull = jax.vjp(layer_norm, hidden_one, vis_gains[1], vis_shifts[1])
    mlp_input = normed_two.astype(BF)
    fc1_pre = dot(mlp_input, fc1_full, 1, 0) + vis_fc1_bias
    fc1_act, gelu_pull = jax.vjp(gelu_tanh, fc1_pre)
    fc1_low = fc1_act.astype(BF)
    fc2_part = dot(fc1_low, fc2_full, 1, 1).reshape(4, sub, wide)
    hidden_sub = lax.dynamic_slice_in_dim(hidden_one, t * sub, sub)
    vision_sub = hidden_sub + sum_tp_quarter(fc2_part) + vis_out_bias[1]
    vision_sub, up_own = lax.optimization_barrier((vision_sub, up_own))
    latent_in = latents.astype(F32)
    latent_low = rms_norm(latent_in, res_gains[1]).astype(BF)
    latent_quarter = lax.dynamic_slice_in_dim(latent_low, t * lsub, lsub)
    latent_quarter = after(latent_quarter, hidden_one)
    latent_cols = share_columns(latent_quarter.reshape(1, lsub, blk, tcol))[0]
    vision_low = place_blocks(ring_gather(vision_sub.astype(BF)))
    vision_low = gather_tp(vision_low).reshape(tokens, wide)
    latent_part = jnp.concatenate(
        [dot(latent_cols, res_q, 1, 0), dot(latent_cols, rkv_own, 1, 0)], axis=1
    )

    gate = dot(vision_low, gate_own, 1, 0)
    up = dot(vision_low, up_own, 1, 0)
    proj_hidden, proj_pull = jax.vjp(swiglu, gate, up)
    proj_ring = ring_gather(proj_hidden.astype(BF))
    pdown = proj_down.reshape(blk, unit, tcol)
    pdown_ring = [lax.dynamic_index_in_dim(pdown, ring_index(k), 0, False) for k in range(blk)]
    context_part = dot(proj_ring[0], pdown_ring[0], 1, 0)
    for k in sorted(range(1, blk), key=lambda k: min(k, blk - k)):
        context_part = context_part + dot(proj_ring[k], pdown_ring[k], 1, 0)
    rout_full = gather_blk_later(after(res_out.T, context_part)).reshape(text, -1)
    quarter = tokens // 4
    context = sum_tp_quarter(context_part.reshape(4, quarter, tcol))
    gain_latent_own = lax.dynamic_slice_in_dim(res_gains[1], b * tcol, tcol)
    gain_context_own = lax.dynamic_slice_in_dim(res_gains[0], b * tcol, tcol)
    scaled_low = (context * gain_context_own).astype(BF)
    kv_part = mm("kc,tcj->tkj", scaled_low, rkv_quad)
    square_part = jnp.sum(context * context, axis=-1)
    high, low = halves(square_part)
    stats = jnp.pad(jnp.stack([high, low], axis=1), ((0, 0), (0, 2 * kvcols - 2)))
    kv_terms = (
        jnp.concatenate([kv_part, stats[None]], axis=0)
        .reshape(5, blk, sub, 2 * kvcols)
        .transpose(1, 2, 0, 3)
        .reshape(blk, sub, -1)
    )
    terms = jnp.concatenate([kv_terms, latent_part.reshape(blk, sub, -1)], axis=2)
    sums = ring_sum(lambda k: lax.dynamic_index_in_dim(terms, ring_index(k), 0, False))
    kv_sums = sums[:, : 10 * kvcols].reshape(sub, 5, 2 * kvcols).transpose(1, 0, 2)
    latent_qkv = sums[:, 10 * kvcols :].reshape(lat, qcols + 2 * kvcols).astype(BF)
    latent_query = latent_qkv[:, :qcols]
    latent_kv = latent_qkv[:, qcols:]
    scale_sub = lax.rsqrt((kv_sums[4, :, 0] + kv_sums[4, :, 1]) / text + EPSILON)
    patch_kv = (kv_sums[:4] * scale_sub[None, :, None]).astype(BF)
    patch_all = exchange(
        jnp.broadcast_to(patch_kv[None], (blk,) + patch_kv.shape).reshape(4 * blk, sub, -1), EVERY
    ).reshape(tokens, 2 * kvcols)

    latent_images = b * (lat // LATENTS) + jnp.arange(lat, dtype=jnp.int32) // LATENTS
    key_images = jnp.concatenate([all_images, latent_images])
    allowed_res = latent_images[:, None] == key_images[None, :]
    res_kv_all = jnp.concatenate([patch_all, latent_kv], axis=0)
    res_key, res_value = res_kv_all[:, :kvcols], res_kv_all[:, kvcols:]
    group = qcols // RES_HEAD
    res_query = latent_query.reshape(lat, group, RES_HEAD)
    res_scale = RES_HEAD ** (-0.5)
    res_scores = mm("qgd,nd->gqn", res_query, res_key) * res_scale
    res_scores = jnp.where(allowed_res[None], res_scores, -jnp.inf)
    res_top = jnp.max(res_scores, axis=-1)
    res_weights = jnp.exp(res_scores - res_top[..., None])
    res_sum = jnp.sum(res_weights, axis=-1)
    res_result = (
        mm("gqn,nd->gqd", res_weights.astype(BF), res_value) / res_sum[..., None]
    ).transpose(1, 0, 2)
    res_lse = res_top + jnp.log(res_sum)
    result_low = res_result.astype(BF).reshape(lat, qcols)

    latent_sub = lax.dynamic_slice_in_dim(latent_in, t * lsub, lsub)
    latent_one = latent_sub + sum_tp_quarter(
        dot(result_low, rout_full, 1, 1).reshape(4, lsub, text)
    )
    kept = jnp.concatenate(
        [query_rows, attn_output, result_low.reshape(tok, -1), fc1_low], axis=1
    )
    kept_all = gather_blk_later(after(kept, latent_one)).reshape(tokens, -1)
    post_normed, post_pull = jax.vjp(rms_norm, latent_one, res_gains[2])
    post_all = gather_rows_every(post_normed.astype(BF))
    gate_up_two = mm("td,dje->tje", post_all, res_gate_up)
    mlp_hidden, mlp_pull = jax.vjp(swiglu, gate_up_two[:, 0], gate_up_two[:, 1])
    mlp_low = mlp_hidden.astype(BF)
    latent_two = latent_one + sum_rows_every(dot(mlp_low, res_down, 1, 0), lsub)
    final_normed, final_pull = jax.vjp(rms_norm, latent_two, res_gains[3])
    grad_sub = lax.dynamic_slice_in_dim(out_grad, t * lsub, lsub).astype(F32)
    dlatent_two, gain_final = final_pull(grad_sub)
    latents_out = gather_tp(final_normed).reshape(lat, text)

    dmlp_all = gather_rows_every(dlatent_two.astype(BF))
    dgate_two, dup_two = mlp_pull(dot(dmlp_all, res_down, 1, 1))
    dgate_up_two = jnp.stack([dgate_two, dup_two], axis=1).astype(BF)
    dpost = sum_rows_every(mm("tje,dje->td", dgate_up_two, res_gate_up), lsub)
    dlatent_part, gain_post = post_pull(dpost)
    dlatent_one = dlatent_two + dlatent_part
    dlatent_one, kept_all = lax.optimization_barrier((dlatent_one, kept_all))
    width, each = heads * HEAD_VIS, lat * qcols // tok
    query_all = kept_all[:, :width].reshape(tokens, heads, HEAD_VIS)
    attn_out_all = kept_all[:, width : 2 * width]
    result_all = kept_all[:, 2 * width : 2 * width + each].reshape(lats, qcols)
    fc1_low_all = kept_all[:, 2 * width + each :]
    dattn_low = gather_tp(dlatent_one.astype(BF)).reshape(lat, text)

    mlp_late, post_late = after(mlp_low, dattn_low), after(post_all, dattn_low)
    grad_res_down = dot(mlp_late, dmlp_all, 0, 0)
    grad_res_gate_up = mm("td,tje->dje", post_late, dgate_up_two)
    dresult = dot(dattn_low, rout_full, 1, 0).astype(BF)
    dresult_heads = dresult.reshape(lat, group, RES_HEAD)
    res_delta = jnp.sum(dresult_heads.astype(F32) * res_result, axis=-1).T
    res_prob = jnp.exp(res_scores - res_lse[..., None])
    dprob = mm("qgd,nd->gqn", dresult_heads, res_value)
    dscores = (res_prob * (dprob - res_delta[..., None])).astype(BF)
    dquery = mm("gqn,nd->qgd", dscores, res_key) * res_scale
    dkey = mm("gqn,qgd->nd", dscores, res_query) * res_scale
    dvalue = mm("gqn,qgd->nd", res_prob.astype(BF), dresult_heads)
    dquery_own = dquery.reshape(lat, qcols).astype(BF)
    dkv_low = jnp.concatenate([dkey, dvalue], axis=1).astype(BF)
    dpatch_local, dlatent_kv = dkv_low[:tokens], dkv_low[tokens:]
    dpatch_sub = jnp.sum(
        exchange(dpatch_local.reshape(4 * blk, sub, 2 * kvcols), EVERY)
        .reshape(blk, 4, sub, 2 * kvcols)
        .astype(F32),
        axis=0,
    )
    dpatch_sub, grad_res_down, grad_res_gate_up = lax.optimization_barrier(
        (dpatch_sub, grad_res_down, grad_res_gate_up)
    )
    grad_res_gate_up = with_layout_constraint(
        grad_res_gate_up, Layout(major_to_minor=(0, 1, 2))
    )
    along = jnp.sum(dpatch_sub * patch_kv.astype(F32), axis=(0, 2)) / text
    a_high, a_low = halves(along)
    s_high, s_low = halves(scale_sub)
    row_stats = jnp.pad(
        jnp.stack([a_high, a_low, s_high, s_low], axis=1), ((0, 0), (0, 2 * kvcols - 4))
    )
    dpatch_rows = gather_blk(jnp.concatenate([dpatch_sub, row_stats[None]], axis=0).astype(BF))
    dpatch_rows, grad_res_gate_up = lax.optimization_barrier((dpatch_rows, grad_res_gate_up))
    dpatch_rows = dpatch_rows.transpose(1, 0, 2, 3).reshape(5, quarter, 2 * kvcols)
    dpatch_quad = dpatch_rows[:4]
    along_rows = dpatch_rows[4, :, 0].astype(F32) + dpatch_rows[4, :, 1].astype(F32)
    scale_rows = dpatch_rows[4, :, 2].astype(F32) + dpatch_rows[4, :, 3].astype(F32)
    dcontext_normed = mm("tkj,tcj->kc", dpatch_quad, rkv_quad)
    unit_context = context * scale_rows[:, None]
    dcontext = scale_rows[:, None] * (
        dcontext_normed * gain_context_own - unit_context * along_rows[:, None]
    )
    gain_context = jnp.sum(dcontext_normed * unit_context, axis=0)
    context_low = (unit_context * gain_context_own).astype(BF)

    dcontext_low = gather_tp(dcontext.astype(BF)).reshape(tokens, tcol)
    arrivals = []
    dproj = ring_sum(lambda k: dot(dcontext_low, pdown_ring[k], 1, 1), arrivals)
    grad_proj_down = jnp.zeros((blk, unit, tcol), F32)
    for k in range(blk):
        block = after(proj_ring[k], arrivals[min(2 * k // blk, len(arrivals) - 1)])
        grad_proj_down = lax.dynamic_update_index_in_dim(
            grad_proj_down, dot(block, dcontext_low, 0, 0), ring_index(k), 0
        )
    grad_proj_down = grad_proj_down.reshape(hidden, tcol)
    res_rows = jnp.concatenate([dquery_own, dlatent_kv], axis=1)
    res_rows = gather_blk(after(res_rows, arrivals[0]))
    res_rows = res_rows.reshape(lats, -1)
    dquery_all, dlkv_all = res_rows[:, :qcols], res_rows[:, qcols:]
    dattn_quarter = after(dlatent_one.astype(BF), arrivals[min(1, len(arrivals) - 1)])
    dattn_cols = share_columns(dattn_quarter.reshape(1, lsub, blk, tcol))[0]
    grad_res_out = dot(result_all, dattn_cols, 0, 0)
    dproj, grad_proj_down, grad_res_out, dquery_all, dlkv_all = lax.optimization_barrier(
        (dproj, grad_proj_down, grad_res_out, dquery_all, dlkv_all)
    )
    dgate, dup = proj_pull(dproj)
    dgate_low, dup_low = dgate.astype(BF), dup.astype(BF)
    dvision_part = dot(dgate_low, gate_own, 1, 1) + dot(dup_low, up_own, 1, 1)
    dvision_sub = sum_every(dvision_part.reshape(4, blk, sub, wide))
    grad_gate = dot(vision_low, dgate_low, 0, 0).astype(BF).reshape(blk, wcol, unit)
    grad_up = dot(vision_low, dup_low, 0, 0).astype(BF).reshape(blk, wcol, unit)
    dvision_sub, grad_gate, grad_up = lax.optimization_barrier((dvision_sub, grad_gate, grad_up))
    dvision_out = gather_tp(dvision_sub).reshape(tok, wide)
    grad_gate = exchange(grad_gate, "blk")

    grad_res_q = dot(latent_cols, dquery_all, 0, 0)
    grad_res_kv = dot(latent_cols, dlkv_all, 0, 0) + sum_tp_quarter(
        mm("kc,tkj->tcj", context_low, dpatch_quad)
    )
    grad_res_kv = grad_res_kv.reshape(tcol, 2, kvcols)
    dlatent_part = dot(dquery_all, res_q, 1, 1) + dot(dlkv_all, rkv_own, 1, 1)
    gain_latent = jnp.sum(dlatent_part * latent_cols.astype(F32), axis=0) / gain_latent_own
    gain_cols = sum_tp(jnp.stack([gain_context, gain_latent]))

    gain_rows = jnp.stack([gain_post, gain_final]).reshape(2, 4, -1).transpose(1, 0, 2)
    gain_rows = sum_tp_quarter(after(gain_rows, dvision_out))
    dfc2_low = dvision_out.astype(BF)
    bias_two = jnp.sum(dfc2_low.astype(F32), axis=0)
    (dfc1_pre,) = gelu_pull(dot(dfc2_low, fc2_full, 1, 0))
    dfc1_low = dfc1_pre.astype(BF)
    bias_fc1 = jnp.sum(dfc1_low.astype(F32), axis=0)
    dnormed_two = sum_tp(dot(dfc1_low, fc1_full, 1, 1))
    dhidden_part, gain_two, shift_two = norm_two_pull(dnormed_two)
    dhidden_one = dvision_out + dhidden_part
    dattn_total = dhidden_one.astype(BF)
    bias_one = jnp.sum(dattn_total.astype(F32), axis=0)
    dattn_output = dot(dattn_total, out_full, 1, 0).astype(BF)
    dattn_output, grad_gate = lax.optimization_barrier((dattn_output, grad_gate))
    dout_heads = dattn_output.reshape(tok, heads, HEAD_VIS)
    vis_delta = jnp.sum(dout_heads.astype(F32) * vis_result, axis=-1)
    d_high, d_low = halves(vis_delta)
    l_high, l_low = halves(vis_lse.T)
    dout_low = jnp.concatenate(
        [dattn_output, jnp.concatenate([d_high, d_low, l_high, l_low], axis=1).astype(BF)], axis=1
    )
    cols = jnp.stack([attn_input, mlp_input, dfc2_low, dattn_total])
    cols = lax.dynamic_slice_in_dim(cols, t * sub, sub, 1)
    cols = cols.reshape(tok, blk, wcol).transpose(1, 0, 2)
    dout_width = dout_low.shape[1]
    dlatent_home = sum_tp_quarter(
        dlatent_part.reshape(blk, 4, lsub, tcol).transpose(1, 0, 2, 3)
    ).astype(BF)
    arrived = exchange(
        jnp.concatenate(
            [
                jnp.broadcast_to(dout_low[None], (blk,) + dout_low.shape),
                cols,
                dlatent_home.reshape(blk, tok, -1),
            ],
            axis=2,
        ),
        "blk",
    )
    dout_all = arrived[:, :, :dout_width].reshape(tokens, -1)
    cols = arrived[:, :, dout_width : dout_width + wcol].reshape(blk, 4, sub, wcol)
    cols = gather_tp(cols).transpose(2, 1, 0, 3, 4).reshape(4, tokens, wcol)
    grad_up = exchange(after(grad_up, dout_all), "blk")
    dfc1_all = gather_blk_later(after(dfc1_low, dout_all)).reshape(tokens, -1)
    dlatent_normed = (
        arrived[:, :, dout_width + wcol :]
        .reshape(blk, lsub, tcol)
        .transpose(1, 0, 2)
        .reshape(lsub, text)
        .astype(F32)
    )
    latent_pull = jax.vjp(rms_norm, latent_sub, res_gains[1])[1]
    dlatent_in, _ = latent_pull(dlatent_normed)
    latents_grad = gather_tp(dlatent_one + dlatent_in).reshape(lat, text)
    row_values = dout_all[:, width:].astype(F32).reshape(tokens, 2, 2, heads).sum(axis=2)
    delta_all, lse_all = row_values[:, 0].T, row_values[:, 1].T
    dout_all_heads = dout_all[:, :width].reshape(tokens, heads, HEAD_VIS)
    prob = jnp.exp(scores - vis_lse[..., None])
    dprob_vis = mm("qhd,khd->hqk", dout_heads, value_all)
    dscores_vis = (prob * (dprob_vis - vis_delta.T[..., None])).astype(BF)
    dquery_home = mm("hqk,khd->qhd", dscores_vis, key_all) * vis_scale
    scores_in = mm("khd,qhd->hkq", key_heads, query_all) * vis_scale
    scores_in = jnp.where(allowed_vis[None], scores_in, -jnp.inf)
    prob_in = jnp.exp(scores_in - lse_all[:, None, :])
    dprob_in = mm("khd,qhd->hkq", value_heads, dout_all_heads)
    dscores_in = (prob_in * (dprob_in - delta_all[:, None, :])).astype(BF)
    dkey_home = mm("hkq,qhd->khd", dscores_in, query_all) * vis_scale
    dvalue_home = mm("hkq,qhd->khd", prob_in.astype(BF), dout_all_heads)
    dqkv_low = jnp.stack(
        [
            dquery_home.reshape(tok, -1),
            dkey_home.reshape(tok, -1),
            dvalue_home.reshape(tok, -1),
        ]
    ).astype(BF)
    dqkv_low, grad_up = lax.optimization_barrier((dqkv_low, grad_up))
    bias_qv = jnp.stack(
        [jnp.sum(dqkv_low[0].astype(F32), axis=0), jnp.sum(dqkv_low[2].astype(F32), axis=0)]
    )
    attn_cols, mlp_cols, dfc2_cols, dattn_vis_cols = (cols[j] for j in range(4))
    dqkv_ring = ring_gather(jnp.concatenate(list(dqkv_low), axis=1))
    dqkv_ring = jnp.concatenate(dqkv_ring, axis=0)
    attn_cols_ring = jnp.concatenate(
        [lax.dynamic_slice_in_dim(attn_cols, ring_index(k) * tok, tok) for k in range(blk)]
    )
    dnormed_one = sum_tp(
        dot(dqkv_low[0], qkv_full[0], 1, 1)
        + dot(dqkv_low[1], qkv_full[1], 1, 1)
        + dot(dqkv_low[2], qkv_full[2], 1, 1)
    )
    dinput_part, gain_one, shift_one = norm_one_pull(dnormed_one)
    patches_grad = dhidden_one + dinput_part

    grad_proj_gate_up = (
        jnp.stack([grad_gate, grad_up]).transpose(2, 0, 1, 3).reshape(wcol, 2, hidden).astype(F32)
    )
    grad_vis_fc2 = dot(dfc2_cols, fc1_low_all, 0, 0).T
    grad_vis_out = dot(dattn_vis_cols, attn_out_all, 0, 0).T
    grad_vis_fc1 = dot(mlp_cols, dfc1_all, 0, 0)
    grad_vis_qkv = dot(attn_cols_ring, dqkv_ring, 0, 0).reshape(wcol, 3, -1)
    small = jnp.concatenate(
        [
            gain_one,
            gain_two,
            shift_one,
            shift_two,
            bias_one,
            bias_two,
            bias_qv.reshape(-1),
            bias_fc1,
            gain_rows.reshape(-1),
            gain_cols.reshape(-1),
        ]
    )
    small = gather_blk(small)
    gain_cols = small[:, small.shape[1] - 2 * tcol :].reshape(blk, 2, tcol)
    small = jnp.sum(small[:, : small.shape[1] - 2 * tcol], axis=0)
    gain_rows = gather_tp(small[small.shape[0] - text // 2 :].reshape(2, text // 4))
    gain_rows = gain_rows.transpose(1, 0, 2).reshape(2, text)
    grad_res_gains = jnp.concatenate([gain_cols.transpose(1, 0, 2).reshape(2, text), gain_rows])
    grad_vis_gains = small[: 2 * wide].reshape(2, wide)
    grad_vis_shifts = small[2 * wide : 4 * wide].reshape(2, wide)
    grad_vis_out_bias = small[4 * wide : 6 * wide].reshape(2, wide)
    grad_vis_qv_bias = small[6 * wide : 6 * wide + 2 * width].reshape(2, width)
    grad_vis_fc1_bias = small[6 * wide + 2 * width : 6 * wide + 2 * width + bias_fc1.shape[0]]
    return (
        latents_out,
        patches_grad,
        latents_grad,
        grad_vis_gains,
        grad_vis_shifts,
        grad_vis_qkv,
        grad_vis_qv_bias,
        grad_vis_out,
        grad_vis_out_bias,
        grad_vis_fc1,
        grad_vis_fc1_bias,
        grad_vis_fc2,
        grad_proj_gate_up,
        grad_proj_down,
        grad_res_gains,
        grad_res_q,
        grad_res_kv,
        grad_res_out,
        grad_res_gate_up,
        grad_res_down,
    )


def solution(mesh):
    placed = (
        P("blk", None),
        P("blk", None),
        P(),
        P(),
        P(),
        P(),
        P("blk", None, "tp"),
        P(None, "tp"),
        P("tp", "blk"),
        P(),
        P("blk", "tp"),
        P("tp"),
        P("tp", "blk"),
        P("blk", None, "tp"),
        P("tp", "blk"),
        P(),
        P("blk", "tp"),
        P("blk", None, "tp"),
        P("tp", "blk"),
        P(None, None, ("blk", "tp")),
        P(("blk", "tp"), None),
        P("blk", None),
    )
    return jax.shard_map(
        per_device,
        mesh=mesh,
        in_specs=placed,
        out_specs=(
            P("blk", None),
            P("blk", None),
            P("blk", None),
            P(),
            P(),
            P("blk", None, "tp"),
            P(None, "tp"),
            P("tp", "blk"),
            P(),
            P("blk", "tp"),
            P("tp"),
            P("tp", "blk"),
            P("blk", None, "tp"),
            P("tp", "blk"),
            P(),
            P("blk", "tp"),
            P("blk", None, "tp"),
            P("tp", "blk"),
            P(None, None, ("blk", "tp")),
            P(("blk", "tp"), None),
        ),
        check_vma=False,
    )
```

```python
import jax
import jax.numpy as jnp
from jax import lax
from jax.experimental import pallas as pl
from jax.experimental.pallas import tpu as pltpu
from jax.sharding import PartitionSpec as P

HEADS = 16
HEAD_VIS = 72
RES_HEAD = 96
LATENTS = 64
EPSILON = 1e-06
EVERY = ("blk", "tp")
BF = jnp.bfloat16
F32 = jnp.float32


def swap_core(value):
    return lax.ppermute(value, "tp", [(i, i ^ 1) for i in range(lax.axis_size("tp"))])


def swap_x(value):
    return lax.ppermute(value, "tp", [(i, i ^ 2) for i in range(lax.axis_size("tp"))])


def my_x():
    return lax.axis_index("tp") // 2


def my_core():
    return lax.axis_index("tp") % 2


def pick(flag, one, zero):
    return jnp.where(flag == 1, one, zero)


def exchange(chunks, axis):
    return lax.all_to_all(chunks, axis, 0, 0, tiled=True)


def gather_direct(value, axis, count):
    return exchange(jnp.broadcast_to(value[None], (count,) + value.shape), axis)


def sum_blk(partial):
    return jnp.sum(exchange(partial.astype(BF), "blk").astype(F32), axis=0)


def sum_tp_quarter(partial):
    pairs = partial.reshape((2, 2) + partial.shape[1:])
    core, x = my_core(), my_x()
    keep = pick(core, pairs[:, 1], pairs[:, 0])
    send = pick(core, pairs[:, 0], pairs[:, 1]).astype(BF)
    half = keep + swap_core(send).astype(F32)
    keep = pick(x, half[1], half[0])
    send = pick(x, half[0], half[1]).astype(BF)
    return keep + swap_x(send).astype(F32)


def gather_tp(value):
    other = swap_x(value)
    x, core = my_x(), my_core()
    both = pick(x, jnp.stack([other, value]), jnp.stack([value, other]))
    far = swap_core(both)
    quad = pick(core, jnp.stack([far, both], axis=1), jnp.stack([both, far], axis=1))
    return quad.reshape((4,) + value.shape)


def sum_tp(partial):
    chip = (partial + swap_core(partial)).astype(BF)
    return chip.astype(F32) + swap_x(chip).astype(F32)


def gather_blk(value):
    return gather_direct(value, "blk", lax.axis_size("blk"))


def gather_blk_later(value):
    return lax.all_gather(value, "blk", axis=0, tiled=False)


def gather_every(value):
    return gather_tp(gather_blk(value))


def sum_every(partial):
    return sum_blk(sum_tp_quarter(partial))


def ring_order():
    count = lax.axis_size("blk")
    return list(range(0, count, 2)) + list(range(count - 1, 0, -2))


def ring_index(distance):
    order = ring_order()
    count = len(order)
    after = [order[(order.index(i) + distance) % count] for i in range(count)]
    return jnp.array(after, jnp.int32)[lax.axis_index("blk")]


def pass_on(value, step):
    order = ring_order()
    count = len(order)
    route = [(order[i], order[(i + step) % count]) for i in range(count)]
    return lax.ppermute(value, "blk", route)


def ring_gather(own):
    count = lax.axis_size("blk")
    half, rows = count // 2, own.shape[0] // 2
    blocks = [own] + [None] * (count - 1)
    ahead = behind = own
    for k in range(1, half):
        behind = pass_on(behind, 1)
        ahead = pass_on(ahead, -1)
        blocks[count - k], blocks[k] = behind, ahead
    blocks[half] = jnp.concatenate(
        [pass_on(behind[:rows], 1), pass_on(ahead[rows:], -1)], axis=0
    )
    return blocks


def ring_sum(part, arrivals=None):
    count = lax.axis_size("blk")
    half = count // 2
    far = part(half)
    rows = far.shape[0] // 2
    low = far.astype(BF)
    onward, back = pass_on(low[:rows], 1), pass_on(low[rows:], -1)
    for k in range(half - 1, 0, -1):
        one, two = part(k), part(count - k)
        if k == half - 1:
            blank = jnp.zeros_like(onward)
            onward = jnp.concatenate([onward, blank], axis=0)
            back = jnp.concatenate([blank, back], axis=0)
        if arrivals is not None:
            arrivals.append(onward)
        onward = pass_on((one + onward.astype(F32)).astype(BF), 1)
        back = pass_on((two + back.astype(F32)).astype(BF), -1)
    return part(0) + onward.astype(F32) + back.astype(F32)


def place_blocks(blocks):
    count = len(blocks)
    order = ring_order()
    table = [[order[(order.index(i) + k) % count] for k in range(count)] for i in range(count)]
    places = lax.dynamic_index_in_dim(
        jnp.array(table, jnp.int32), lax.axis_index("blk"), 0, False
    )

    def kernel(places_ref, *refs):
        for k in range(count):
            refs[count][places_ref[k]] = refs[k][...]

    return pl.pallas_call(
        kernel,
        out_shape=jax.ShapeDtypeStruct((count,) + blocks[0].shape, blocks[0].dtype),
        in_specs=[pl.BlockSpec(memory_space=pltpu.SMEM)]
        + [pl.BlockSpec(memory_space=pltpu.VMEM)] * count,
        out_specs=pl.BlockSpec(memory_space=pltpu.VMEM),
        compiler_params=pltpu.CompilerParams(vmem_limit_bytes=24 * 2**20),
        name="place_blocks",
    )(places, *blocks)


def share_columns(rows):
    parts, own, count, width = rows.shape
    got = gather_tp(exchange(rows.transpose(2, 0, 1, 3), "blk"))
    return got.transpose(2, 1, 0, 3, 4).reshape(parts, count * 4 * own, width)


def after(value, *others):
    return lax.optimization_barrier((value,) + others)[0]


def ring_groups():
    count = lax.axis_size("blk")
    half = count // 2
    return [[0]] + [[k, count - k] for k in range(1, half)] + [[half]]


def gather_rows_every(own):
    blocks = ring_gather(own)
    parts = []
    for group in ring_groups():
        parts.append(gather_tp(jnp.concatenate([blocks[k] for k in group], axis=0)))
    return jnp.concatenate([part.reshape((-1,) + own.shape[1:]) for part in parts], axis=0)


def sum_rows_every(partial, rows):
    start, sums = 0, {}
    pieces = []
    for group in ring_groups():
        size = 4 * len(group) * rows
        pieces.append((group, partial[start : start + size]))
        start += size
    for group, piece in reversed(pieces):
        total = sum_tp_quarter(piece.reshape((4, len(group) * rows) + partial.shape[1:]))
        for place, k in enumerate(group):
            sums[k] = total[place * rows : (place + 1) * rows]
    return ring_sum(lambda k: sums[k])


def layer_norm(values, gain, shift):
    center = values - jnp.mean(values, axis=-1, keepdims=True)
    spread = jnp.mean(center * center, axis=-1, keepdims=True)
    return center * lax.rsqrt(spread + EPSILON) * gain + shift


def rms_norm(values, gain):
    return values * lax.rsqrt(jnp.mean(values * values, axis=-1, keepdims=True) + EPSILON) * gain


def gelu_tanh(values):
    return jax.nn.gelu(values, approximate=True)


def swiglu(gate_part, up_part):
    return jax.nn.silu(gate_part) * up_part


def mm(spec, left, right):
    return jnp.einsum(spec, left, right, preferred_element_type=F32)


def dot(left, right, on_left, on_right):
    return lax.dot_general(
        left, right, (((on_left,), (on_right,)), ((), ())), preferred_element_type=F32
    )


def halves(value):
    high = lax.reduce_precision(value, 8, 7)
    return high, lax.reduce_precision(value - high, 8, 7)


def stream_images(image_patches, span_order, tok_rows):
    bounds = jnp.cumsum(image_patches)
    rows = span_order[:, None] * tok_rows + jnp.arange(tok_rows, dtype=jnp.int32)[None, :]
    stream = rows.reshape(-1)
    return jnp.sum((stream[:, None] >= bounds[None, :]).astype(jnp.int32), axis=1)


def wide_gradient(left, gate, up):
    rows, wide = left.shape
    cols = gate.shape[1]
    tile = 512

    def kernel(left_ref, gate_ref, up_ref, out_ref):
        part = left_ref[...]
        out_ref[:, 0, :] = dot(part, gate_ref[...], 0, 0)
        out_ref[:, 1, :] = dot(part, up_ref[...], 0, 0)

    return pl.pallas_call(
        kernel,
        grid=(wide // tile,),
        out_shape=jax.ShapeDtypeStruct((wide, 2, cols), F32),
        in_specs=[
            pl.BlockSpec((rows, tile), lambda i: (0, i)),
            pl.BlockSpec((rows, cols), lambda i: (0, 0)),
            pl.BlockSpec((rows, cols), lambda i: (0, 0)),
        ],
        out_specs=pl.BlockSpec((tile, 2, cols), lambda i: (i, 0, 0)),
        compiler_params=pltpu.CompilerParams(vmem_limit_bytes=40 * 2**20),
        cost_estimate=pl.CostEstimate(
            flops=4 * rows * wide * cols,
            bytes_accessed=2 * rows * (wide + 2 * cols) + 8 * wide * cols,
            transcendentals=0,
        ),
        name="wide_gradient",
    )(left, gate, up)


def per_device(
    patches,
    latents,
    image_patches,
    span_order,
    vis_gains,
    vis_shifts,
    vis_qkv,
    vis_qv_bias,
    vis_out,
    vis_out_bias,
    vis_fc1,
    vis_fc1_bias,
    vis_fc2,
    proj_gate_up,
    proj_down,
    res_gains,
    res_q,
    res_kv,
    res_out,
    res_gate_up,
    res_down,
    out_grad,
):
    blk = lax.axis_size("blk")
    b, t = lax.axis_index("blk"), lax.axis_index("tp")
    tok, wide = patches.shape
    lat, text = latents.shape
    sub, lsub = tok // 4, lat // 4
    tokens, lats = tok * blk, lat * blk
    wcol, tcol = wide // blk, text // blk
    heads = HEADS // 4
    unit = proj_down.shape[0] // blk
    hidden = proj_down.shape[0]
    qcols = res_q.shape[1]
    kvcols = RES_HEAD

    attn_shard = jnp.concatenate([vis_qkv.transpose(1, 0, 2), vis_out.T[None]], axis=0)
    attn_ring = ring_gather(attn_shard)
    attn_full = place_blocks(attn_ring)
    gu_chunks = proj_gate_up.reshape(wcol, 2, blk, unit).transpose(2, 1, 0, 3)
    gate_chunks, up_chunks = gu_chunks[:, 0], gu_chunks[:, 1]
    attn_full, gate_chunks, up_chunks = lax.optimization_barrier(
        (attn_full, gate_chunks, up_chunks)
    )
    attn_full = attn_full.transpose(1, 0, 2, 3).reshape(4, wide, -1)
    qkv_full, out_full = attn_full[:3], attn_full[3]
    fc1_full = gather_blk_later(vis_fc1).reshape(wide, -1)
    fc2_full = gather_blk_later(vis_fc2.T).reshape(wide, -1)
    rkv_own = res_kv.reshape(tcol, 2 * kvcols)
    rkv_quad = gather_tp(rkv_own)

    all_images = stream_images(image_patches, span_order, tok)
    own_images = lax.dynamic_slice_in_dim(all_images, b * tok, tok)
    allowed_vis = own_images[:, None] == all_images[None, :]
    inputs = patches.astype(F32)
    normed_one, norm_one_pull = jax.vjp(layer_norm, inputs, vis_gains[0], vis_shifts[0])
    attn_input = normed_one.astype(BF)
    query_rows = (dot(attn_input, qkv_full[0], 1, 0) + vis_qv_bias[0]).astype(BF)
    key_rows = dot(attn_input, qkv_full[1], 1, 0).astype(BF)
    value_rows = (dot(attn_input, qkv_full[2], 1, 0) + vis_qv_bias[1]).astype(BF)
    kv_all = jnp.stack(ring_gather(jnp.concatenate([key_rows, value_rows], axis=1)))
    key_all = kv_all[:, :, : heads * HEAD_VIS].reshape(tokens, heads, HEAD_VIS)
    value_all = kv_all[:, :, heads * HEAD_VIS :].reshape(tokens, heads, HEAD_VIS)
    ring_images = jnp.stack(
        [all_images.reshape(blk, tok)[ring_index(k)] for k in range(blk)]
    ).reshape(-1)
    allowed_ring = own_images[:, None] == ring_images[None, :]
    query_heads = query_rows.reshape(tok, heads, HEAD_VIS)
    key_heads = key_rows.reshape(tok, heads, HEAD_VIS)
    value_heads = value_rows.reshape(tok, heads, HEAD_VIS)
    vis_scale = HEAD_VIS ** (-0.5)
    scores = mm("qhd,khd->hqk", query_heads, key_all) * vis_scale
    scores = jnp.where(allowed_ring[None], scores, -jnp.inf)
    row_top = jnp.max(scores, axis=-1)
    weights = jnp.exp(scores - row_top[..., None])
    weight_sum = jnp.sum(weights, axis=-1)
    weighted = mm("hqk,khd->hqd", weights.astype(BF), value_all)
    vis_lse = row_top + jnp.log(weight_sum)
    vis_result = (weighted / weight_sum[..., None]).transpose(1, 0, 2)
    attn_output = vis_result.astype(BF).reshape(tok, -1)

    gate_own = exchange(after(gate_chunks, kv_all), "blk").reshape(wide, unit)
    up_own = exchange(after(up_chunks, gate_own), "blk").reshape(wide, unit)

    hidden_one = inputs + sum_tp(dot(attn_output, out_full, 1, 1)) + vis_out_bias[0]
    hidden_one, gate_own = lax.optimization_barrier((hidden_one, gate_own))
    normed_two, norm_two_pull = jax.vjp(layer_norm, hidden_one, vis_gains[1], vis_shifts[1])
    mlp_input = normed_two.astype(BF)
    fc1_pre = dot(mlp_input, fc1_full, 1, 0) + vis_fc1_bias
    fc1_act, gelu_pull = jax.vjp(gelu_tanh, fc1_pre)
    fc1_low = fc1_act.astype(BF)
    fc2_part = dot(fc1_low, fc2_full, 1, 1).reshape(4, sub, wide)
    hidden_sub = lax.dynamic_slice_in_dim(hidden_one, t * sub, sub)
    vision_sub = hidden_sub + sum_tp_quarter(fc2_part) + vis_out_bias[1]
    vision_sub, up_own = lax.optimization_barrier((vision_sub, up_own))
    latent_in = latents.astype(F32)
    latent_low = rms_norm(latent_in, res_gains[1]).astype(BF)
    latent_quarter = lax.dynamic_slice_in_dim(latent_low, t * lsub, lsub)
    latent_quarter = after(latent_quarter, hidden_one)
    latent_cols = share_columns(latent_quarter.reshape(1, lsub, blk, tcol))[0]
    vision_low = place_blocks(ring_gather(vision_sub.astype(BF)))
    vision_low = gather_tp(vision_low).reshape(tokens, wide)
    latent_part = jnp.concatenate(
        [dot(latent_cols, res_q, 1, 0), dot(latent_cols, rkv_own, 1, 0)], axis=1
    )

    gate = dot(vision_low, gate_own, 1, 0)
    up = dot(vision_low, up_own, 1, 0)
    proj_hidden, proj_pull = jax.vjp(swiglu, gate, up)
    proj_ring = ring_gather(proj_hidden.astype(BF))
    pdown = proj_down.reshape(blk, unit, tcol)
    pdown_ring = [lax.dynamic_index_in_dim(pdown, ring_index(k), 0, False) for k in range(blk)]
    context_part = dot(proj_ring[0], pdown_ring[0], 1, 0)
    for k in sorted(range(1, blk), key=lambda k: min(k, blk - k)):
        context_part = context_part + dot(proj_ring[k], pdown_ring[k], 1, 0)
    rout_full = gather_blk_later(after(res_out.T, context_part)).reshape(text, -1)
    quarter = tokens // 4
    context = sum_tp_quarter(context_part.reshape(4, quarter, tcol))
    gain_latent_own = lax.dynamic_slice_in_dim(res_gains[1], b * tcol, tcol)
    gain_context_own = lax.dynamic_slice_in_dim(res_gains[0], b * tcol, tcol)
    scaled_low = (context * gain_context_own).astype(BF)
    kv_part = mm("kc,tcj->tkj", scaled_low, rkv_quad)
    square_part = jnp.sum(context * context, axis=-1)
    high, low = halves(square_part)
    stats = jnp.pad(jnp.stack([high, low], axis=1), ((0, 0), (0, 2 * kvcols - 2)))
    kv_terms = (
        jnp.concatenate([kv_part, stats[None]], axis=0)
        .reshape(5, blk, sub, 2 * kvcols)
        .transpose(1, 2, 0, 3)
        .reshape(blk, sub, -1)
    )
    terms = jnp.concatenate([kv_terms, latent_part.reshape(blk, sub, -1)], axis=2)
    sums = ring_sum(lambda k: lax.dynamic_index_in_dim(terms, ring_index(k), 0, False))
    kv_sums = sums[:, : 10 * kvcols].reshape(sub, 5, 2 * kvcols).transpose(1, 0, 2)
    latent_qkv = sums[:, 10 * kvcols :].reshape(lat, qcols + 2 * kvcols).astype(BF)
    latent_query = latent_qkv[:, :qcols]
    latent_kv = latent_qkv[:, qcols:]
    scale_sub = lax.rsqrt((kv_sums[4, :, 0] + kv_sums[4, :, 1]) / text + EPSILON)
    patch_kv = (kv_sums[:4] * scale_sub[None, :, None]).astype(BF)
    patch_all = exchange(
        jnp.broadcast_to(patch_kv[None], (blk,) + patch_kv.shape).reshape(4 * blk, sub, -1), EVERY
    ).reshape(tokens, 2 * kvcols)

    latent_images = b * (lat // LATENTS) + jnp.arange(lat, dtype=jnp.int32) // LATENTS
    key_images = jnp.concatenate([all_images, latent_images])
    allowed_res = latent_images[:, None] == key_images[None, :]
    res_kv_all = jnp.concatenate([patch_all, latent_kv], axis=0)
    res_key, res_value = res_kv_all[:, :kvcols], res_kv_all[:, kvcols:]
    group = qcols // RES_HEAD
    res_query = latent_query.reshape(lat, group, RES_HEAD)
    res_scale = RES_HEAD ** (-0.5)
    res_scores = mm("qgd,nd->gqn", res_query, res_key) * res_scale
    res_scores = jnp.where(allowed_res[None], res_scores, -jnp.inf)
    res_top = jnp.max(res_scores, axis=-1)
    res_weights = jnp.exp(res_scores - res_top[..., None])
    res_sum = jnp.sum(res_weights, axis=-1)
    res_result = (
        mm("gqn,nd->gqd", res_weights.astype(BF), res_value) / res_sum[..., None]
    ).transpose(1, 0, 2)
    res_lse = res_top + jnp.log(res_sum)
    result_low = res_result.astype(BF).reshape(lat, qcols)

    latent_sub = lax.dynamic_slice_in_dim(latent_in, t * lsub, lsub)
    latent_one = latent_sub + sum_tp_quarter(
        dot(result_low, rout_full, 1, 1).reshape(4, lsub, text)
    )
    kept = jnp.concatenate(
        [query_rows, attn_output, result_low.reshape(tok, -1), fc1_low], axis=1
    )
    kept_all = gather_blk_later(after(kept, latent_one)).reshape(tokens, -1)
    post_normed, post_pull = jax.vjp(rms_norm, latent_one, res_gains[2])
    post_all = gather_rows_every(post_normed.astype(BF))
    gate_up_two = mm("td,dje->tje", post_all, res_gate_up)
    mlp_hidden, mlp_pull = jax.vjp(swiglu, gate_up_two[:, 0], gate_up_two[:, 1])
    mlp_low = mlp_hidden.astype(BF)
    latent_two = latent_one + sum_rows_every(dot(mlp_low, res_down, 1, 0), lsub)
    final_normed, final_pull = jax.vjp(rms_norm, latent_two, res_gains[3])
    grad_sub = lax.dynamic_slice_in_dim(out_grad, t * lsub, lsub).astype(F32)
    dlatent_two, gain_final = final_pull(grad_sub)
    latents_out = gather_tp(final_normed).reshape(lat, text)

    dmlp_all = gather_rows_every(dlatent_two.astype(BF))
    dgate_two, dup_two = mlp_pull(dot(dmlp_all, res_down, 1, 1))
    dgate_up_two = jnp.stack([dgate_two, dup_two], axis=1).astype(BF)
    dpost = sum_rows_every(mm("tje,dje->td", dgate_up_two, res_gate_up), lsub)
    dlatent_part, gain_post = post_pull(dpost)
    dlatent_one = dlatent_two + dlatent_part
    dlatent_one, kept_all = lax.optimization_barrier((dlatent_one, kept_all))
    width, each = heads * HEAD_VIS, lat * qcols // tok
    query_all = kept_all[:, :width].reshape(tokens, heads, HEAD_VIS)
    attn_out_all = kept_all[:, width : 2 * width]
    result_all = kept_all[:, 2 * width : 2 * width + each].reshape(lats, qcols)
    fc1_low_all = kept_all[:, 2 * width + each :]
    dattn_low = gather_tp(dlatent_one.astype(BF)).reshape(lat, text)

    mlp_late, post_late = after(mlp_low, dattn_low), after(post_all, dattn_low)
    grad_res_down = dot(mlp_late, dmlp_all, 0, 0)
    grad_res_gate_up = wide_gradient(post_late, dgate_up_two[:, 0], dgate_up_two[:, 1])
    dresult = dot(dattn_low, rout_full, 1, 0).astype(BF)
    dresult_heads = dresult.reshape(lat, group, RES_HEAD)
    res_delta = jnp.sum(dresult_heads.astype(F32) * res_result, axis=-1).T
    res_prob = jnp.exp(res_scores - res_lse[..., None])
    dprob = mm("qgd,nd->gqn", dresult_heads, res_value)
    dscores = (res_prob * (dprob - res_delta[..., None])).astype(BF)
    dquery = mm("gqn,nd->qgd", dscores, res_key) * res_scale
    dkey = mm("gqn,qgd->nd", dscores, res_query) * res_scale
    dvalue = mm("gqn,qgd->nd", res_prob.astype(BF), dresult_heads)
    dquery_own = dquery.reshape(lat, qcols).astype(BF)
    dkv_low = jnp.concatenate([dkey, dvalue], axis=1).astype(BF)
    dpatch_local, dlatent_kv = dkv_low[:tokens], dkv_low[tokens:]
    dpatch_sub = jnp.sum(
        exchange(dpatch_local.reshape(4 * blk, sub, 2 * kvcols), EVERY)
        .reshape(blk, 4, sub, 2 * kvcols)
        .astype(F32),
        axis=0,
    )
    dpatch_sub, grad_res_gate_up = lax.optimization_barrier((dpatch_sub, grad_res_gate_up))
    along = jnp.sum(dpatch_sub * patch_kv.astype(F32), axis=(0, 2)) / text
    a_high, a_low = halves(along)
    s_high, s_low = halves(scale_sub)
    row_stats = jnp.pad(
        jnp.stack([a_high, a_low, s_high, s_low], axis=1), ((0, 0), (0, 2 * kvcols - 4))
    )
    dpatch_rows = gather_blk(jnp.concatenate([dpatch_sub, row_stats[None]], axis=0).astype(BF))
    dpatch_rows, grad_res_down = lax.optimization_barrier((dpatch_rows, grad_res_down))
    dpatch_rows = dpatch_rows.transpose(1, 0, 2, 3).reshape(5, quarter, 2 * kvcols)
    dpatch_quad = dpatch_rows[:4]
    along_rows = dpatch_rows[4, :, 0].astype(F32) + dpatch_rows[4, :, 1].astype(F32)
    scale_rows = dpatch_rows[4, :, 2].astype(F32) + dpatch_rows[4, :, 3].astype(F32)
    dcontext_normed = mm("tkj,tcj->kc", dpatch_quad, rkv_quad)
    unit_context = context * scale_rows[:, None]
    dcontext = scale_rows[:, None] * (
        dcontext_normed * gain_context_own - unit_context * along_rows[:, None]
    )
    gain_context = jnp.sum(dcontext_normed * unit_context, axis=0)
    context_low = (unit_context * gain_context_own).astype(BF)

    dcontext_low = gather_tp(dcontext.astype(BF)).reshape(tokens, tcol)
    arrivals = []
    dproj = ring_sum(lambda k: dot(dcontext_low, pdown_ring[k], 1, 1), arrivals)
    grad_proj_down = jnp.zeros((blk, unit, tcol), F32)
    for k in range(blk):
        block = after(proj_ring[k], arrivals[min(2 * k // blk, len(arrivals) - 1)])
        grad_proj_down = lax.dynamic_update_index_in_dim(
            grad_proj_down, dot(block, dcontext_low, 0, 0), ring_index(k), 0
        )
    grad_proj_down = grad_proj_down.reshape(hidden, tcol)
    res_rows = jnp.concatenate([dquery_own, dlatent_kv], axis=1)
    res_rows = gather_blk(after(res_rows, arrivals[0]))
    res_rows = res_rows.reshape(lats, -1)
    dquery_all, dlkv_all = res_rows[:, :qcols], res_rows[:, qcols:]
    dattn_quarter = after(dlatent_one.astype(BF), arrivals[min(1, len(arrivals) - 1)])
    dattn_cols = share_columns(dattn_quarter.reshape(1, lsub, blk, tcol))[0]
    grad_res_out = dot(result_all, dattn_cols, 0, 0)
    dproj, grad_proj_down, grad_res_out, dquery_all, dlkv_all = lax.optimization_barrier(
        (dproj, grad_proj_down, grad_res_out, dquery_all, dlkv_all)
    )
    dgate, dup = proj_pull(dproj)
    dgate_low, dup_low = dgate.astype(BF), dup.astype(BF)
    dvision_part = dot(dgate_low, gate_own, 1, 1) + dot(dup_low, up_own, 1, 1)
    dvision_sub = sum_every(dvision_part.reshape(4, blk, sub, wide))
    grad_gate = dot(vision_low, dgate_low, 0, 0).astype(BF).reshape(blk, wcol, unit)
    grad_up = dot(vision_low, dup_low, 0, 0).astype(BF).reshape(blk, wcol, unit)
    dvision_sub, grad_gate, grad_up = lax.optimization_barrier((dvision_sub, grad_gate, grad_up))
    dvision_out = gather_tp(dvision_sub).reshape(tok, wide)
    grad_gate = exchange(grad_gate, "blk")

    grad_res_q = dot(latent_cols, dquery_all, 0, 0)
    grad_res_kv = dot(latent_cols, dlkv_all, 0, 0) + sum_tp_quarter(
        mm("kc,tkj->tcj", context_low, dpatch_quad)
    )
    grad_res_kv = grad_res_kv.reshape(tcol, 2, kvcols)
    dlatent_part = dot(dquery_all, res_q, 1, 1) + dot(dlkv_all, rkv_own, 1, 1)
    gain_latent = jnp.sum(dlatent_part * latent_cols.astype(F32), axis=0) / gain_latent_own
    gain_cols = sum_tp(jnp.stack([gain_context, gain_latent]))

    gain_rows = jnp.stack([gain_post, gain_final]).reshape(2, 4, -1).transpose(1, 0, 2)
    gain_rows = sum_tp_quarter(after(gain_rows, dvision_out))
    dfc2_low = dvision_out.astype(BF)
    bias_two = jnp.sum(dfc2_low.astype(F32), axis=0)
    (dfc1_pre,) = gelu_pull(dot(dfc2_low, fc2_full, 1, 0))
    dfc1_low = dfc1_pre.astype(BF)
    bias_fc1 = jnp.sum(dfc1_low.astype(F32), axis=0)
    dnormed_two = sum_tp(dot(dfc1_low, fc1_full, 1, 1))
    dhidden_part, gain_two, shift_two = norm_two_pull(dnormed_two)
    dhidden_one = dvision_out + dhidden_part
    dattn_total = dhidden_one.astype(BF)
    bias_one = jnp.sum(dattn_total.astype(F32), axis=0)
    dattn_output = dot(dattn_total, out_full, 1, 0).astype(BF)
    dattn_output, grad_gate = lax.optimization_barrier((dattn_output, grad_gate))
    dout_heads = dattn_output.reshape(tok, heads, HEAD_VIS)
    vis_delta = jnp.sum(dout_heads.astype(F32) * vis_result, axis=-1)
    d_high, d_low = halves(vis_delta)
    l_high, l_low = halves(vis_lse.T)
    dout_low = jnp.concatenate(
        [dattn_output, jnp.concatenate([d_high, d_low, l_high, l_low], axis=1).astype(BF)], axis=1
    )
    cols = jnp.stack([attn_input, mlp_input, dfc2_low, dattn_total])
    cols = lax.dynamic_slice_in_dim(cols, t * sub, sub, 1)
    cols = cols.reshape(tok, blk, wcol).transpose(1, 0, 2)
    dout_width = dout_low.shape[1]
    dlatent_home = sum_tp_quarter(
        dlatent_part.reshape(blk, 4, lsub, tcol).transpose(1, 0, 2, 3)
    ).astype(BF)
    arrived = exchange(
        jnp.concatenate(
            [
                jnp.broadcast_to(dout_low[None], (blk,) + dout_low.shape),
                cols,
                dlatent_home.reshape(blk, tok, -1),
            ],
            axis=2,
        ),
        "blk",
    )
    dout_all = arrived[:, :, :dout_width].reshape(tokens, -1)
    cols = arrived[:, :, dout_width : dout_width + wcol].reshape(blk, 4, sub, wcol)
    cols = gather_tp(cols).transpose(2, 1, 0, 3, 4).reshape(4, tokens, wcol)
    grad_up = exchange(after(grad_up, dout_all), "blk")
    dfc1_all = gather_blk_later(after(dfc1_low, dout_all)).reshape(tokens, -1)
    dlatent_normed = (
        arrived[:, :, dout_width + wcol :]
        .reshape(blk, lsub, tcol)
        .transpose(1, 0, 2)
        .reshape(lsub, text)
        .astype(F32)
    )
    latent_pull = jax.vjp(rms_norm, latent_sub, res_gains[1])[1]
    dlatent_in, _ = latent_pull(dlatent_normed)
    latents_grad = gather_tp(dlatent_one + dlatent_in).reshape(lat, text)
    row_values = dout_all[:, width:].astype(F32).reshape(tokens, 2, 2, heads).sum(axis=2)
    delta_all, lse_all = row_values[:, 0].T, row_values[:, 1].T
    dout_all_heads = dout_all[:, :width].reshape(tokens, heads, HEAD_VIS)
    prob = jnp.exp(scores - vis_lse[..., None])
    dprob_vis = mm("qhd,khd->hqk", dout_heads, value_all)
    dscores_vis = (prob * (dprob_vis - vis_delta.T[..., None])).astype(BF)
    dquery_home = mm("hqk,khd->qhd", dscores_vis, key_all) * vis_scale
    scores_in = mm("khd,qhd->hkq", key_heads, query_all) * vis_scale
    scores_in = jnp.where(allowed_vis[None], scores_in, -jnp.inf)
    prob_in = jnp.exp(scores_in - lse_all[:, None, :])
    dprob_in = mm("khd,qhd->hkq", value_heads, dout_all_heads)
    dscores_in = (prob_in * (dprob_in - delta_all[:, None, :])).astype(BF)
    dkey_home = mm("hkq,qhd->khd", dscores_in, query_all) * vis_scale
    dvalue_home = mm("hkq,qhd->khd", prob_in.astype(BF), dout_all_heads)
    dqkv_low = jnp.stack(
        [
            dquery_home.reshape(tok, -1),
            dkey_home.reshape(tok, -1),
            dvalue_home.reshape(tok, -1),
        ]
    ).astype(BF)
    dqkv_low, grad_up = lax.optimization_barrier((dqkv_low, grad_up))
    bias_qv = jnp.stack(
        [jnp.sum(dqkv_low[0].astype(F32), axis=0), jnp.sum(dqkv_low[2].astype(F32), axis=0)]
    )
    attn_cols, mlp_cols, dfc2_cols, dattn_vis_cols = (cols[j] for j in range(4))
    dqkv_ring = ring_gather(jnp.concatenate(list(dqkv_low), axis=1))
    dqkv_ring = jnp.concatenate(dqkv_ring, axis=0)
    attn_cols_ring = jnp.concatenate(
        [lax.dynamic_slice_in_dim(attn_cols, ring_index(k) * tok, tok) for k in range(blk)]
    )
    dnormed_one = sum_tp(
        dot(dqkv_low[0], qkv_full[0], 1, 1)
        + dot(dqkv_low[1], qkv_full[1], 1, 1)
        + dot(dqkv_low[2], qkv_full[2], 1, 1)
    )
    dinput_part, gain_one, shift_one = norm_one_pull(dnormed_one)
    patches_grad = dhidden_one + dinput_part

    grad_proj_gate_up = (
        jnp.stack([grad_gate, grad_up]).transpose(2, 0, 1, 3).reshape(wcol, 2, hidden).astype(F32)
    )
    grad_vis_fc2 = dot(dfc2_cols, fc1_low_all, 0, 0).T
    grad_vis_out = dot(dattn_vis_cols, attn_out_all, 0, 0).T
    grad_vis_fc1 = dot(mlp_cols, dfc1_all, 0, 0)
    grad_vis_qkv = dot(attn_cols_ring, dqkv_ring, 0, 0).reshape(wcol, 3, -1)
    small = jnp.concatenate(
        [
            gain_one,
            gain_two,
            shift_one,
            shift_two,
            bias_one,
            bias_two,
            bias_qv.reshape(-1),
            bias_fc1,
            gain_rows.reshape(-1),
            gain_cols.reshape(-1),
        ]
    )
    small = gather_blk(small)
    gain_cols = small[:, small.shape[1] - 2 * tcol :].reshape(blk, 2, tcol)
    small = jnp.sum(small[:, : small.shape[1] - 2 * tcol], axis=0)
    gain_rows = gather_tp(small[small.shape[0] - text // 2 :].reshape(2, text // 4))
    gain_rows = gain_rows.transpose(1, 0, 2).reshape(2, text)
    grad_res_gains = jnp.concatenate([gain_cols.transpose(1, 0, 2).reshape(2, text), gain_rows])
    grad_vis_gains = small[: 2 * wide].reshape(2, wide)
    grad_vis_shifts = small[2 * wide : 4 * wide].reshape(2, wide)
    grad_vis_out_bias = small[4 * wide : 6 * wide].reshape(2, wide)
    grad_vis_qv_bias = small[6 * wide : 6 * wide + 2 * width].reshape(2, width)
    grad_vis_fc1_bias = small[6 * wide + 2 * width : 6 * wide + 2 * width + bias_fc1.shape[0]]
    return (
        latents_out,
        patches_grad,
        latents_grad,
        grad_vis_gains,
        grad_vis_shifts,
        grad_vis_qkv,
        grad_vis_qv_bias,
        grad_vis_out,
        grad_vis_out_bias,
        grad_vis_fc1,
        grad_vis_fc1_bias,
        grad_vis_fc2,
        grad_proj_gate_up,
        grad_proj_down,
        grad_res_gains,
        grad_res_q,
        grad_res_kv,
        grad_res_out,
        grad_res_gate_up,
        grad_res_down,
    )


def solution(mesh):
    placed = (
        P("blk", None),
        P("blk", None),
        P(),
        P(),
        P(),
        P(),
        P("blk", None, "tp"),
        P(None, "tp"),
        P("tp", "blk"),
        P(),
        P("blk", "tp"),
        P("tp"),
        P("tp", "blk"),
        P("blk", None, "tp"),
        P("tp", "blk"),
        P(),
        P("blk", "tp"),
        P("blk", None, "tp"),
        P("tp", "blk"),
        P(None, None, ("blk", "tp")),
        P(("blk", "tp"), None),
        P("blk", None),
    )
    return jax.shard_map(
        per_device,
        mesh=mesh,
        in_specs=placed,
        out_specs=(
            P("blk", None),
            P("blk", None),
            P("blk", None),
            P(),
            P(),
            P("blk", None, "tp"),
            P(None, "tp"),
            P("tp", "blk"),
            P(),
            P("blk", "tp"),
            P("tp"),
            P("tp", "blk"),
            P("blk", None, "tp"),
            P("tp", "blk"),
            P(),
            P("blk", "tp"),
            P("blk", None, "tp"),
            P("tp", "blk"),
            P(None, None, ("blk", "tp")),
            P(("blk", "tp"), None),
        ),
        check_vma=False,
    )
```

```python
import jax
import jax.numpy as jnp
from jax import lax
from jax.experimental import pallas as pl
from jax.experimental.pallas import tpu as pltpu
from jax.sharding import PartitionSpec as P

HEADS = 16
HEAD_VIS = 72
RES_HEAD = 96
LATENTS = 64
EPSILON = 1e-06
EVERY = ("blk", "tp")
BF = jnp.bfloat16
F32 = jnp.float32


def swap_core(value):
    return lax.ppermute(value, "tp", [(i, i ^ 1) for i in range(lax.axis_size("tp"))])


def swap_x(value):
    return lax.ppermute(value, "tp", [(i, i ^ 2) for i in range(lax.axis_size("tp"))])


def my_x():
    return lax.axis_index("tp") // 2


def my_core():
    return lax.axis_index("tp") % 2


def pick(flag, one, zero):
    return jnp.where(flag == 1, one, zero)


def exchange(chunks, axis):
    return lax.all_to_all(chunks, axis, 0, 0, tiled=True)


def gather_direct(value, axis, count):
    return exchange(jnp.broadcast_to(value[None], (count,) + value.shape), axis)


def sum_blk(partial):
    return jnp.sum(exchange(partial.astype(BF), "blk").astype(F32), axis=0)


def sum_tp_quarter(partial):
    pairs = partial.reshape((2, 2) + partial.shape[1:])
    core, x = my_core(), my_x()
    keep = pick(core, pairs[:, 1], pairs[:, 0])
    send = pick(core, pairs[:, 0], pairs[:, 1]).astype(BF)
    half = keep + swap_core(send).astype(F32)
    keep = pick(x, half[1], half[0])
    send = pick(x, half[0], half[1]).astype(BF)
    return keep + swap_x(send).astype(F32)


def gather_tp(value):
    other = swap_x(value)
    x, core = my_x(), my_core()
    both = pick(x, jnp.stack([other, value]), jnp.stack([value, other]))
    far = swap_core(both)
    quad = pick(core, jnp.stack([far, both], axis=1), jnp.stack([both, far], axis=1))
    return quad.reshape((4,) + value.shape)


def sum_tp(partial):
    chip = (partial + swap_core(partial)).astype(BF)
    return chip.astype(F32) + swap_x(chip).astype(F32)


def gather_blk(value):
    return gather_direct(value, "blk", lax.axis_size("blk"))


def gather_blk_later(value):
    return lax.all_gather(value, "blk", axis=0, tiled=False)


def gather_every(value):
    return gather_tp(gather_blk(value))


def sum_every(partial):
    return sum_blk(sum_tp_quarter(partial))


def ring_order():
    count = lax.axis_size("blk")
    return list(range(0, count, 2)) + list(range(count - 1, 0, -2))


def ring_index(distance):
    order = ring_order()
    count = len(order)
    after = [order[(order.index(i) + distance) % count] for i in range(count)]
    return jnp.array(after, jnp.int32)[lax.axis_index("blk")]


def pass_on(value, step):
    order = ring_order()
    count = len(order)
    route = [(order[i], order[(i + step) % count]) for i in range(count)]
    return lax.ppermute(value, "blk", route)


def ring_gather(own):
    count = lax.axis_size("blk")
    half, rows = count // 2, own.shape[0] // 2
    blocks = [own] + [None] * (count - 1)
    ahead = behind = own
    for k in range(1, half):
        behind = pass_on(behind, 1)
        ahead = pass_on(ahead, -1)
        blocks[count - k], blocks[k] = behind, ahead
    blocks[half] = jnp.concatenate(
        [pass_on(behind[:rows], 1), pass_on(ahead[rows:], -1)], axis=0
    )
    return blocks


def ring_sum(part, arrivals=None):
    count = lax.axis_size("blk")
    half = count // 2
    far = part(half)
    rows = far.shape[0] // 2
    low = far.astype(BF)
    onward, back = pass_on(low[:rows], 1), pass_on(low[rows:], -1)
    for k in range(half - 1, 0, -1):
        one, two = part(k), part(count - k)
        if k == half - 1:
            blank = jnp.zeros_like(onward)
            onward = jnp.concatenate([onward, blank], axis=0)
            back = jnp.concatenate([blank, back], axis=0)
        if arrivals is not None:
            arrivals.append(onward)
        onward = pass_on((one + onward.astype(F32)).astype(BF), 1)
        back = pass_on((two + back.astype(F32)).astype(BF), -1)
    return part(0) + onward.astype(F32) + back.astype(F32)


def place_blocks(blocks):
    count = len(blocks)
    order = ring_order()
    table = [[order[(order.index(i) + k) % count] for k in range(count)] for i in range(count)]
    places = lax.dynamic_index_in_dim(
        jnp.array(table, jnp.int32), lax.axis_index("blk"), 0, False
    )

    def kernel(places_ref, *refs):
        for k in range(count):
            refs[count][places_ref[k]] = refs[k][...]

    return pl.pallas_call(
        kernel,
        out_shape=jax.ShapeDtypeStruct((count,) + blocks[0].shape, blocks[0].dtype),
        in_specs=[pl.BlockSpec(memory_space=pltpu.SMEM)]
        + [pl.BlockSpec(memory_space=pltpu.VMEM)] * count,
        out_specs=pl.BlockSpec(memory_space=pltpu.VMEM),
        compiler_params=pltpu.CompilerParams(vmem_limit_bytes=24 * 2**20),
        name="place_blocks",
    )(places, *blocks)


def share_columns(rows):
    parts, own, count, width = rows.shape
    got = gather_tp(exchange(rows.transpose(2, 0, 1, 3), "blk"))
    return got.transpose(2, 1, 0, 3, 4).reshape(parts, count * 4 * own, width)


def after(value, *others):
    return lax.optimization_barrier((value,) + others)[0]


def ring_groups():
    count = lax.axis_size("blk")
    half = count // 2
    return [[0]] + [[k, count - k] for k in range(1, half)] + [[half]]


def gather_rows_every(own):
    blocks = ring_gather(own)
    parts = []
    for group in ring_groups():
        parts.append(gather_tp(jnp.concatenate([blocks[k] for k in group], axis=0)))
    return jnp.concatenate([part.reshape((-1,) + own.shape[1:]) for part in parts], axis=0)


def sum_rows_every(partial, rows):
    start, sums = 0, {}
    pieces = []
    for group in ring_groups():
        size = 4 * len(group) * rows
        pieces.append((group, partial[start : start + size]))
        start += size
    for group, piece in reversed(pieces):
        total = sum_tp_quarter(piece.reshape((4, len(group) * rows) + partial.shape[1:]))
        for place, k in enumerate(group):
            sums[k] = total[place * rows : (place + 1) * rows]
    return ring_sum(lambda k: sums[k])


def layer_norm(values, gain, shift):
    center = values - jnp.mean(values, axis=-1, keepdims=True)
    spread = jnp.mean(center * center, axis=-1, keepdims=True)
    return center * lax.rsqrt(spread + EPSILON) * gain + shift


def rms_norm(values, gain):
    return values * lax.rsqrt(jnp.mean(values * values, axis=-1, keepdims=True) + EPSILON) * gain


def gelu_tanh(values):
    return jax.nn.gelu(values, approximate=True)


def swiglu(gate_part, up_part):
    return jax.nn.silu(gate_part) * up_part


def mm(spec, left, right):
    return jnp.einsum(spec, left, right, preferred_element_type=F32)


def dot(left, right, on_left, on_right):
    return lax.dot_general(
        left, right, (((on_left,), (on_right,)), ((), ())), preferred_element_type=F32
    )


def halves(value):
    high = lax.reduce_precision(value, 8, 7)
    return high, lax.reduce_precision(value - high, 8, 7)


def stream_images(image_patches, span_order, tok_rows):
    bounds = jnp.cumsum(image_patches)
    rows = span_order[:, None] * tok_rows + jnp.arange(tok_rows, dtype=jnp.int32)[None, :]
    stream = rows.reshape(-1)
    return jnp.sum((stream[:, None] >= bounds[None, :]).astype(jnp.int32), axis=1)


def wide_gradient(left, gate, up):
    rows, wide = left.shape
    cols = gate.shape[1]
    tile = 512

    def kernel(left_ref, gate_ref, up_ref, out_ref):
        part = left_ref[...]
        out_ref[:, 0, :] = dot(part, gate_ref[...], 0, 0)
        out_ref[:, 1, :] = dot(part, up_ref[...], 0, 0)

    return pl.pallas_call(
        kernel,
        grid=(wide // tile,),
        out_shape=jax.ShapeDtypeStruct((wide, 2, cols), F32),
        in_specs=[
            pl.BlockSpec((rows, tile), lambda i: (0, i)),
            pl.BlockSpec((rows, cols), lambda i: (0, 0)),
            pl.BlockSpec((rows, cols), lambda i: (0, 0)),
        ],
        out_specs=pl.BlockSpec((tile, 2, cols), lambda i: (i, 0, 0)),
        compiler_params=pltpu.CompilerParams(vmem_limit_bytes=40 * 2**20),
        cost_estimate=pl.CostEstimate(
            flops=4 * rows * wide * cols,
            bytes_accessed=2 * rows * (wide + 2 * cols) + 8 * wide * cols,
            transcendentals=0,
        ),
        name="wide_gradient",
    )(left, gate, up)


def per_device(
    patches,
    latents,
    image_patches,
    span_order,
    vis_gains,
    vis_shifts,
    vis_qkv,
    vis_qv_bias,
    vis_out,
    vis_out_bias,
    vis_fc1,
    vis_fc1_bias,
    vis_fc2,
    proj_gate_up,
    proj_down,
    res_gains,
    res_q,
    res_kv,
    res_out,
    res_gate_up,
    res_down,
    out_grad,
):
    blk = lax.axis_size("blk")
    b, t = lax.axis_index("blk"), lax.axis_index("tp")
    tok, wide = patches.shape
    lat, text = latents.shape
    sub, lsub = tok // 4, lat // 4
    tokens, lats = tok * blk, lat * blk
    wcol, tcol = wide // blk, text // blk
    heads = HEADS // 4
    unit = proj_down.shape[0] // blk
    hidden = proj_down.shape[0]
    qcols = res_q.shape[1]
    kvcols = RES_HEAD

    attn_shard = jnp.concatenate([vis_qkv.transpose(1, 0, 2), vis_out.T[None]], axis=0)
    attn_ring = ring_gather(attn_shard)
    attn_full = place_blocks(attn_ring)
    gu_chunks = proj_gate_up.reshape(wcol, 2, blk, unit).transpose(2, 1, 0, 3)
    gate_chunks, up_chunks = gu_chunks[:, 0], gu_chunks[:, 1]
    attn_full, gate_chunks, up_chunks = lax.optimization_barrier(
        (attn_full, gate_chunks, up_chunks)
    )
    attn_full = attn_full.transpose(1, 0, 2, 3).reshape(4, wide, -1)
    qkv_full, out_full = attn_full[:3], attn_full[3]
    fc1_full = gather_blk_later(vis_fc1).reshape(wide, -1)
    fc2_full = gather_blk_later(vis_fc2.T).reshape(wide, -1)
    rkv_own = res_kv.reshape(tcol, 2 * kvcols)
    rkv_quad = gather_tp(rkv_own)

    all_images = stream_images(image_patches, span_order, tok)
    own_images = lax.dynamic_slice_in_dim(all_images, b * tok, tok)
    allowed_vis = own_images[:, None] == all_images[None, :]
    inputs = patches.astype(F32)
    normed_one, norm_one_pull = jax.vjp(layer_norm, inputs, vis_gains[0], vis_shifts[0])
    attn_input = normed_one.astype(BF)
    query_rows = (dot(attn_input, qkv_full[0], 1, 0) + vis_qv_bias[0]).astype(BF)
    key_rows = dot(attn_input, qkv_full[1], 1, 0).astype(BF)
    value_rows = (dot(attn_input, qkv_full[2], 1, 0) + vis_qv_bias[1]).astype(BF)
    kv_all = jnp.stack(ring_gather(jnp.concatenate([key_rows, value_rows], axis=1)))
    key_all = kv_all[:, :, : heads * HEAD_VIS].reshape(tokens, heads, HEAD_VIS)
    value_all = kv_all[:, :, heads * HEAD_VIS :].reshape(tokens, heads, HEAD_VIS)
    ring_images = jnp.stack(
        [all_images.reshape(blk, tok)[ring_index(k)] for k in range(blk)]
    ).reshape(-1)
    allowed_ring = own_images[:, None] == ring_images[None, :]
    query_heads = query_rows.reshape(tok, heads, HEAD_VIS)
    key_heads = key_rows.reshape(tok, heads, HEAD_VIS)
    value_heads = value_rows.reshape(tok, heads, HEAD_VIS)
    vis_scale = HEAD_VIS ** (-0.5)
    scores = mm("qhd,khd->hqk", query_heads, key_all) * vis_scale
    scores = jnp.where(allowed_ring[None], scores, -jnp.inf)
    row_top = jnp.max(scores, axis=-1)
    weights = jnp.exp(scores - row_top[..., None])
    weight_sum = jnp.sum(weights, axis=-1)
    weighted = mm("hqk,khd->hqd", weights.astype(BF), value_all)
    vis_lse = row_top + jnp.log(weight_sum)
    vis_result = (weighted / weight_sum[..., None]).transpose(1, 0, 2)
    attn_output = vis_result.astype(BF).reshape(tok, -1)

    gate_own = exchange(after(gate_chunks, kv_all), "blk").reshape(wide, unit)
    up_own = exchange(after(up_chunks, gate_own), "blk").reshape(wide, unit)

    hidden_one = inputs + sum_tp(dot(attn_output, out_full, 1, 1)) + vis_out_bias[0]
    hidden_one, gate_own = lax.optimization_barrier((hidden_one, gate_own))
    normed_two, norm_two_pull = jax.vjp(layer_norm, hidden_one, vis_gains[1], vis_shifts[1])
    mlp_input = normed_two.astype(BF)
    fc1_pre = dot(mlp_input, fc1_full, 1, 0) + vis_fc1_bias
    fc1_act, gelu_pull = jax.vjp(gelu_tanh, fc1_pre)
    fc1_low = fc1_act.astype(BF)
    fc2_part = dot(fc1_low, fc2_full, 1, 1).reshape(4, sub, wide)
    hidden_sub = lax.dynamic_slice_in_dim(hidden_one, t * sub, sub)
    vision_sub = hidden_sub + sum_tp_quarter(fc2_part) + vis_out_bias[1]
    vision_sub, up_own = lax.optimization_barrier((vision_sub, up_own))
    latent_in = latents.astype(F32)
    latent_low = rms_norm(latent_in, res_gains[1]).astype(BF)
    latent_quarter = lax.dynamic_slice_in_dim(latent_low, t * lsub, lsub)
    latent_quarter = after(latent_quarter, hidden_one)
    latent_cols = share_columns(latent_quarter.reshape(1, lsub, blk, tcol))[0]
    vision_low = place_blocks(ring_gather(vision_sub.astype(BF)))
    vision_low = gather_tp(vision_low).reshape(tokens, wide)
    latent_part = jnp.concatenate(
        [dot(latent_cols, res_q, 1, 0), dot(latent_cols, rkv_own, 1, 0)], axis=1
    )

    gate = dot(vision_low, gate_own, 1, 0)
    up = dot(vision_low, up_own, 1, 0)
    proj_hidden, proj_pull = jax.vjp(swiglu, gate, up)
    proj_ring = ring_gather(proj_hidden.astype(BF))
    pdown = proj_down.reshape(blk, unit, tcol)
    pdown_ring = [lax.dynamic_index_in_dim(pdown, ring_index(k), 0, False) for k in range(blk)]
    context_part = dot(proj_ring[0], pdown_ring[0], 1, 0)
    for k in sorted(range(1, blk), key=lambda k: min(k, blk - k)):
        context_part = context_part + dot(proj_ring[k], pdown_ring[k], 1, 0)
    rout_full = gather_blk_later(after(res_out.T, context_part)).reshape(text, -1)
    quarter = tokens // 4
    context = sum_tp_quarter(context_part.reshape(4, quarter, tcol))
    gain_latent_own = lax.dynamic_slice_in_dim(res_gains[1], b * tcol, tcol)
    gain_context_own = lax.dynamic_slice_in_dim(res_gains[0], b * tcol, tcol)
    scaled_low = (context * gain_context_own).astype(BF)
    kv_part = mm("kc,tcj->tkj", scaled_low, rkv_quad)
    square_part = jnp.sum(context * context, axis=-1)
    high, low = halves(square_part)
    stats = jnp.pad(jnp.stack([high, low], axis=1), ((0, 0), (0, 2 * kvcols - 2)))
    kv_terms = (
        jnp.concatenate([kv_part, stats[None]], axis=0)
        .reshape(5, blk, sub, 2 * kvcols)
        .transpose(1, 2, 0, 3)
        .reshape(blk, sub, -1)
    )
    terms = jnp.concatenate([kv_terms, latent_part.reshape(blk, sub, -1)], axis=2)
    sums = ring_sum(lambda k: lax.dynamic_index_in_dim(terms, ring_index(k), 0, False))
    kv_sums = sums[:, : 10 * kvcols].reshape(sub, 5, 2 * kvcols).transpose(1, 0, 2)
    latent_qkv = sums[:, 10 * kvcols :].reshape(lat, qcols + 2 * kvcols).astype(BF)
    latent_query = latent_qkv[:, :qcols]
    latent_kv = latent_qkv[:, qcols:]
    scale_sub = lax.rsqrt((kv_sums[4, :, 0] + kv_sums[4, :, 1]) / text + EPSILON)
    patch_kv = (kv_sums[:4] * scale_sub[None, :, None]).astype(BF)
    patch_all = exchange(
        jnp.broadcast_to(patch_kv[None], (blk,) + patch_kv.shape).reshape(4 * blk, sub, -1), EVERY
    ).reshape(tokens, 2 * kvcols)

    latent_images = b * (lat // LATENTS) + jnp.arange(lat, dtype=jnp.int32) // LATENTS
    key_images = jnp.concatenate([all_images, latent_images])
    allowed_res = latent_images[:, None] == key_images[None, :]
    res_kv_all = jnp.concatenate([patch_all, latent_kv], axis=0)
    res_key, res_value = res_kv_all[:, :kvcols], res_kv_all[:, kvcols:]
    group = qcols // RES_HEAD
    res_query = latent_query.reshape(lat, group, RES_HEAD)
    res_scale = RES_HEAD ** (-0.5)
    res_scores = mm("qgd,nd->gqn", res_query, res_key) * res_scale
    res_scores = jnp.where(allowed_res[None], res_scores, -jnp.inf)
    res_top = jnp.max(res_scores, axis=-1)
    res_weights = jnp.exp(res_scores - res_top[..., None])
    res_sum = jnp.sum(res_weights, axis=-1)
    res_result = (
        mm("gqn,nd->gqd", res_weights.astype(BF), res_value) / res_sum[..., None]
    ).transpose(1, 0, 2)
    res_lse = res_top + jnp.log(res_sum)
    result_low = res_result.astype(BF).reshape(lat, qcols)

    latent_sub = lax.dynamic_slice_in_dim(latent_in, t * lsub, lsub)
    latent_one = latent_sub + sum_tp_quarter(
        dot(result_low, rout_full, 1, 1).reshape(4, lsub, text)
    )
    kept = jnp.concatenate(
        [query_rows, attn_output, result_low.reshape(tok, -1), fc1_low], axis=1
    )
    kept_all = gather_blk_later(after(kept, latent_one)).reshape(tokens, -1)
    post_normed, post_pull = jax.vjp(rms_norm, latent_one, res_gains[2])
    post_all = gather_rows_every(post_normed.astype(BF))
    gate_up_two = mm("td,dje->tje", post_all, res_gate_up)
    mlp_hidden, mlp_pull = jax.vjp(swiglu, gate_up_two[:, 0], gate_up_two[:, 1])
    mlp_low = mlp_hidden.astype(BF)
    latent_two = latent_one + sum_rows_every(dot(mlp_low, res_down, 1, 0), lsub)
    final_normed, final_pull = jax.vjp(rms_norm, latent_two, res_gains[3])
    grad_sub = lax.dynamic_slice_in_dim(out_grad, t * lsub, lsub).astype(F32)
    dlatent_two, gain_final = final_pull(grad_sub)
    latents_out = gather_tp(final_normed).reshape(lat, text)

    dmlp_all = gather_rows_every(dlatent_two.astype(BF))
    dgate_two, dup_two = mlp_pull(dot(dmlp_all, res_down, 1, 1))
    dgate_up_two = jnp.stack([dgate_two, dup_two], axis=1).astype(BF)
    dpost = sum_rows_every(mm("tje,dje->td", dgate_up_two, res_gate_up), lsub)
    dlatent_part, gain_post = post_pull(dpost)
    dlatent_one = dlatent_two + dlatent_part
    dlatent_one, kept_all = lax.optimization_barrier((dlatent_one, kept_all))
    width, each = heads * HEAD_VIS, lat * qcols // tok
    query_all = kept_all[:, :width].reshape(tokens, heads, HEAD_VIS)
    attn_out_all = kept_all[:, width : 2 * width]
    result_all = kept_all[:, 2 * width : 2 * width + each].reshape(lats, qcols)
    fc1_low_all = kept_all[:, 2 * width + each :]
    dattn_low = gather_tp(dlatent_one.astype(BF)).reshape(lat, text)

    mlp_late, post_late = after(mlp_low, dattn_low), after(post_all, dattn_low)
    grad_res_down = dot(mlp_late, dmlp_all, 0, 0)
    grad_res_gate_up = wide_gradient(post_late, dgate_up_two[:, 0], dgate_up_two[:, 1])
    dresult = dot(dattn_low, rout_full, 1, 0).astype(BF)
    dresult_heads = dresult.reshape(lat, group, RES_HEAD)
    res_delta = jnp.sum(dresult_heads.astype(F32) * res_result, axis=-1).T
    res_prob = jnp.exp(res_scores - res_lse[..., None])
    dprob = mm("qgd,nd->gqn", dresult_heads, res_value)
    dscores = (res_prob * (dprob - res_delta[..., None])).astype(BF)
    dquery = mm("gqn,nd->qgd", dscores, res_key) * res_scale
    dkey = mm("gqn,qgd->nd", dscores, res_query) * res_scale
    dvalue = mm("gqn,qgd->nd", res_prob.astype(BF), dresult_heads)
    dquery_own = dquery.reshape(lat, qcols).astype(BF)
    dkv_low = jnp.concatenate([dkey, dvalue], axis=1).astype(BF)
    dpatch_local, dlatent_kv = dkv_low[:tokens], dkv_low[tokens:]
    dpatch_sub = jnp.sum(
        exchange(dpatch_local.reshape(4 * blk, sub, 2 * kvcols), EVERY)
        .reshape(blk, 4, sub, 2 * kvcols)
        .astype(F32),
        axis=0,
    )
    dpatch_sub, grad_res_gate_up = lax.optimization_barrier((dpatch_sub, grad_res_gate_up))
    along = jnp.sum(dpatch_sub * patch_kv.astype(F32), axis=(0, 2)) / text
    a_high, a_low = halves(along)
    s_high, s_low = halves(scale_sub)
    row_stats = jnp.pad(
        jnp.stack([a_high, a_low, s_high, s_low], axis=1), ((0, 0), (0, 2 * kvcols - 4))
    )
    dpatch_rows = gather_blk(jnp.concatenate([dpatch_sub, row_stats[None]], axis=0).astype(BF))
    dpatch_rows, grad_res_down = lax.optimization_barrier((dpatch_rows, grad_res_down))
    dpatch_rows = dpatch_rows.transpose(1, 0, 2, 3).reshape(5, quarter, 2 * kvcols)
    dpatch_quad = dpatch_rows[:4]
    along_rows = dpatch_rows[4, :, 0].astype(F32) + dpatch_rows[4, :, 1].astype(F32)
    scale_rows = dpatch_rows[4, :, 2].astype(F32) + dpatch_rows[4, :, 3].astype(F32)
    dcontext_normed = mm("tkj,tcj->kc", dpatch_quad, rkv_quad)
    unit_context = context * scale_rows[:, None]
    dcontext = scale_rows[:, None] * (
        dcontext_normed * gain_context_own - unit_context * along_rows[:, None]
    )
    gain_context = jnp.sum(dcontext_normed * unit_context, axis=0)
    context_low = (unit_context * gain_context_own).astype(BF)

    dcontext_low = gather_tp(dcontext.astype(BF)).reshape(tokens, tcol)
    arrivals = []
    dproj = ring_sum(lambda k: dot(dcontext_low, pdown_ring[k], 1, 1), arrivals)
    grad_proj_down = jnp.zeros((blk, unit, tcol), F32)
    for k in range(blk):
        block = after(proj_ring[k], arrivals[min(2 * k // blk, len(arrivals) - 1)])
        grad_proj_down = lax.dynamic_update_index_in_dim(
            grad_proj_down, dot(block, dcontext_low, 0, 0), ring_index(k), 0
        )
    grad_proj_down = grad_proj_down.reshape(hidden, tcol)
    res_rows = jnp.concatenate([dquery_own, dlatent_kv], axis=1)
    res_rows = gather_blk(after(res_rows, arrivals[0]))
    res_rows = res_rows.reshape(lats, -1)
    dquery_all, dlkv_all = res_rows[:, :qcols], res_rows[:, qcols:]
    dattn_quarter = after(dlatent_one.astype(BF), arrivals[min(1, len(arrivals) - 1)])
    dattn_cols = share_columns(dattn_quarter.reshape(1, lsub, blk, tcol))[0]
    grad_res_out = dot(result_all, dattn_cols, 0, 0)
    dproj, grad_proj_down, grad_res_out, dquery_all, dlkv_all = lax.optimization_barrier(
        (dproj, grad_proj_down, grad_res_out, dquery_all, dlkv_all)
    )
    dgate, dup = proj_pull(dproj)
    dgate_low, dup_low = dgate.astype(BF), dup.astype(BF)
    dvision_part = dot(dgate_low, gate_own, 1, 1) + dot(dup_low, up_own, 1, 1)
    dvision_sub = sum_every(dvision_part.reshape(4, blk, sub, wide))
    grad_gate = dot(vision_low, dgate_low, 0, 0).astype(BF).reshape(blk, wcol, unit)
    dvision_sub, grad_gate = lax.optimization_barrier((dvision_sub, grad_gate))
    dup_late = after(dup_low, dvision_sub)
    grad_up = dot(vision_low, dup_late, 0, 0).astype(BF).reshape(blk, wcol, unit)
    dvision_out = gather_tp(dvision_sub).reshape(tok, wide)
    grad_gate = exchange(grad_gate, "blk")

    grad_res_q = dot(latent_cols, dquery_all, 0, 0)
    grad_res_kv = dot(latent_cols, dlkv_all, 0, 0) + sum_tp_quarter(
        mm("kc,tkj->tcj", context_low, dpatch_quad)
    )
    grad_res_kv = grad_res_kv.reshape(tcol, 2, kvcols)
    dlatent_part = dot(dquery_all, res_q, 1, 1) + dot(dlkv_all, rkv_own, 1, 1)
    gain_latent = jnp.sum(dlatent_part * latent_cols.astype(F32), axis=0) / gain_latent_own
    gain_cols = sum_tp(jnp.stack([gain_context, gain_latent]))

    gain_rows = jnp.stack([gain_post, gain_final]).reshape(2, 4, -1).transpose(1, 0, 2)
    gain_rows = sum_tp_quarter(after(gain_rows, dvision_out))
    dfc2_low = dvision_out.astype(BF)
    bias_two = jnp.sum(dfc2_low.astype(F32), axis=0)
    (dfc1_pre,) = gelu_pull(dot(dfc2_low, fc2_full, 1, 0))
    dfc1_low = dfc1_pre.astype(BF)
    bias_fc1 = jnp.sum(dfc1_low.astype(F32), axis=0)
    dnormed_two = sum_tp(dot(dfc1_low, fc1_full, 1, 1))
    dhidden_part, gain_two, shift_two = norm_two_pull(dnormed_two)
    dhidden_one = dvision_out + dhidden_part
    dattn_total = dhidden_one.astype(BF)
    bias_one = jnp.sum(dattn_total.astype(F32), axis=0)
    dattn_output = dot(dattn_total, out_full, 1, 0).astype(BF)
    dattn_output, grad_gate = lax.optimization_barrier((dattn_output, grad_gate))
    dout_heads = dattn_output.reshape(tok, heads, HEAD_VIS)
    vis_delta = jnp.sum(dout_heads.astype(F32) * vis_result, axis=-1)
    d_high, d_low = halves(vis_delta)
    l_high, l_low = halves(vis_lse.T)
    dout_low = jnp.concatenate(
        [dattn_output, jnp.concatenate([d_high, d_low, l_high, l_low], axis=1).astype(BF)], axis=1
    )
    cols = jnp.stack([attn_input, mlp_input, dfc2_low, dattn_total])
    cols = lax.dynamic_slice_in_dim(cols, t * sub, sub, 1)
    cols = cols.reshape(tok, blk, wcol).transpose(1, 0, 2)
    dout_width = dout_low.shape[1]
    dlatent_home = sum_tp_quarter(
        dlatent_part.reshape(blk, 4, lsub, tcol).transpose(1, 0, 2, 3)
    ).astype(BF)
    arrived = exchange(
        jnp.concatenate(
            [
                jnp.broadcast_to(dout_low[None], (blk,) + dout_low.shape),
                cols,
                dlatent_home.reshape(blk, tok, -1),
            ],
            axis=2,
        ),
        "blk",
    )
    dout_all = arrived[:, :, :dout_width].reshape(tokens, -1)
    cols = arrived[:, :, dout_width : dout_width + wcol].reshape(blk, 4, sub, wcol)
    cols = gather_tp(cols).transpose(2, 1, 0, 3, 4).reshape(4, tokens, wcol)
    grad_up = exchange(after(grad_up, dout_all), "blk")
    dfc1_all = gather_blk_later(after(dfc1_low, dout_all)).reshape(tokens, -1)
    dlatent_normed = (
        arrived[:, :, dout_width + wcol :]
        .reshape(blk, lsub, tcol)
        .transpose(1, 0, 2)
        .reshape(lsub, text)
        .astype(F32)
    )
    latent_pull = jax.vjp(rms_norm, latent_sub, res_gains[1])[1]
    dlatent_in, _ = latent_pull(dlatent_normed)
    latents_grad = gather_tp(dlatent_one + dlatent_in).reshape(lat, text)
    row_values = dout_all[:, width:].astype(F32).reshape(tokens, 2, 2, heads).sum(axis=2)
    delta_all, lse_all = row_values[:, 0].T, row_values[:, 1].T
    dout_all_heads = dout_all[:, :width].reshape(tokens, heads, HEAD_VIS)
    prob = jnp.exp(scores - vis_lse[..., None])
    dprob_vis = mm("qhd,khd->hqk", dout_heads, value_all)
    dscores_vis = (prob * (dprob_vis - vis_delta.T[..., None])).astype(BF)
    dquery_home = mm("hqk,khd->qhd", dscores_vis, key_all) * vis_scale
    scores_in = mm("khd,qhd->hkq", key_heads, query_all) * vis_scale
    scores_in = jnp.where(allowed_vis[None], scores_in, -jnp.inf)
    prob_in = jnp.exp(scores_in - lse_all[:, None, :])
    dprob_in = mm("khd,qhd->hkq", value_heads, dout_all_heads)
    dscores_in = (prob_in * (dprob_in - delta_all[:, None, :])).astype(BF)
    dkey_home = mm("hkq,qhd->khd", dscores_in, query_all) * vis_scale
    dvalue_home = mm("hkq,qhd->khd", prob_in.astype(BF), dout_all_heads)
    dqkv_low = jnp.stack(
        [
            dquery_home.reshape(tok, -1),
            dkey_home.reshape(tok, -1),
            dvalue_home.reshape(tok, -1),
        ]
    ).astype(BF)
    dqkv_low, grad_up = lax.optimization_barrier((dqkv_low, grad_up))
    bias_qv = jnp.stack(
        [jnp.sum(dqkv_low[0].astype(F32), axis=0), jnp.sum(dqkv_low[2].astype(F32), axis=0)]
    )
    attn_cols, mlp_cols, dfc2_cols, dattn_vis_cols = (cols[j] for j in range(4))
    dqkv_ring = ring_gather(jnp.concatenate(list(dqkv_low), axis=1))
    dqkv_ring = jnp.concatenate(dqkv_ring, axis=0)
    attn_cols_ring = jnp.concatenate(
        [lax.dynamic_slice_in_dim(attn_cols, ring_index(k) * tok, tok) for k in range(blk)]
    )
    dnormed_one = sum_tp(
        dot(dqkv_low[0], qkv_full[0], 1, 1)
        + dot(dqkv_low[1], qkv_full[1], 1, 1)
        + dot(dqkv_low[2], qkv_full[2], 1, 1)
    )
    dinput_part, gain_one, shift_one = norm_one_pull(dnormed_one)
    patches_grad = dhidden_one + dinput_part

    grad_proj_gate_up = (
        jnp.stack([grad_gate, grad_up]).transpose(2, 0, 1, 3).reshape(wcol, 2, hidden).astype(F32)
    )
    grad_vis_fc2 = dot(dfc2_cols, fc1_low_all, 0, 0).T
    grad_vis_out = dot(dattn_vis_cols, attn_out_all, 0, 0).T
    grad_vis_fc1 = dot(mlp_cols, dfc1_all, 0, 0)
    grad_vis_qkv = dot(attn_cols_ring, dqkv_ring, 0, 0).reshape(wcol, 3, -1)
    small = jnp.concatenate(
        [
            gain_one,
            gain_two,
            shift_one,
            shift_two,
            bias_one,
            bias_two,
            bias_qv.reshape(-1),
            bias_fc1,
            gain_rows.reshape(-1),
            gain_cols.reshape(-1),
        ]
    )
    small = gather_blk(small)
    gain_cols = small[:, small.shape[1] - 2 * tcol :].reshape(blk, 2, tcol)
    small = jnp.sum(small[:, : small.shape[1] - 2 * tcol], axis=0)
    gain_rows = gather_tp(small[small.shape[0] - text // 2 :].reshape(2, text // 4))
    gain_rows = gain_rows.transpose(1, 0, 2).reshape(2, text)
    grad_res_gains = jnp.concatenate([gain_cols.transpose(1, 0, 2).reshape(2, text), gain_rows])
    grad_vis_gains = small[: 2 * wide].reshape(2, wide)
    grad_vis_shifts = small[2 * wide : 4 * wide].reshape(2, wide)
    grad_vis_out_bias = small[4 * wide : 6 * wide].reshape(2, wide)
    grad_vis_qv_bias = small[6 * wide : 6 * wide + 2 * width].reshape(2, width)
    grad_vis_fc1_bias = small[6 * wide + 2 * width : 6 * wide + 2 * width + bias_fc1.shape[0]]
    return (
        latents_out,
        patches_grad,
        latents_grad,
        grad_vis_gains,
        grad_vis_shifts,
        grad_vis_qkv,
        grad_vis_qv_bias,
        grad_vis_out,
        grad_vis_out_bias,
        grad_vis_fc1,
        grad_vis_fc1_bias,
        grad_vis_fc2,
        grad_proj_gate_up,
        grad_proj_down,
        grad_res_gains,
        grad_res_q,
        grad_res_kv,
        grad_res_out,
        grad_res_gate_up,
        grad_res_down,
    )


def solution(mesh):
    placed = (
        P("blk", None),
        P("blk", None),
        P(),
        P(),
        P(),
        P(),
        P("blk", None, "tp"),
        P(None, "tp"),
        P("tp", "blk"),
        P(),
        P("blk", "tp"),
        P("tp"),
        P("tp", "blk"),
        P("blk", None, "tp"),
        P("tp", "blk"),
        P(),
        P("blk", "tp"),
        P("blk", None, "tp"),
        P("tp", "blk"),
        P(None, None, ("blk", "tp")),
        P(("blk", "tp"), None),
        P("blk", None),
    )
    return jax.shard_map(
        per_device,
        mesh=mesh,
        in_specs=placed,
        out_specs=(
            P("blk", None),
            P("blk", None),
            P("blk", None),
            P(),
            P(),
            P("blk", None, "tp"),
            P(None, "tp"),
            P("tp", "blk"),
            P(),
            P("blk", "tp"),
            P("tp"),
            P("tp", "blk"),
            P("blk", None, "tp"),
            P("tp", "blk"),
            P(),
            P("blk", "tp"),
            P("blk", None, "tp"),
            P("tp", "blk"),
            P(None, None, ("blk", "tp")),
            P(("blk", "tp"), None),
        ),
        check_vma=False,
    )
```
